256 devices in a mesh: row: 16 (over x, y), col: 16 (over z, core).
Axes of the slice: x: 4, y: 4, z: 8, core: 2. Of those that a mesh axis runs over, the one named last changes fastest.
Arguments:
- tiles: float32 [16, 16, 3, 128, 64, 128], P('row', 'col'), may hold values from -0.0625 to 0.0625
- tile_coords: int32 [16, 16, 3, 2, 256], P('row', 'col'), may hold values from 0 to 31, as said below
- tile_count: int32 [16, 16, 3], P('row', 'col'), may hold values from 32 to 256, as said below
- seeds: int32 [128], replicated, may hold values from 0 to 32767
- chain: int32 [3], replicated, may hold values from 0 to 2
Outputs:
- answers: float32 [32768, 128], P(('row', 'col'))
The draws below stay inside these ranges and needn't reach their ends.
Inputs may be any that keep to these rules, and one draw needn't show every extreme that they name: tile_coords[..., 0, :] is below 16 * 2 and tile_coords[..., 1, :] below 16 * 2; pairs may repeat. `tile_count`: each count is 256 divided by 1, 2, 4 or 8; for every relation some device has all 256 slots live.
All inputs are finite; a program needn't handle non-finite values.
Results may differ from the reference program's by a relative error of at most 0.0003.
Values sent between devices are 32-bit elements; how exact they have to be, the bound alone decides.
A program may use at most 128 MiB of HBM per device.

```python
import jax
import jax.numpy as jnp
from jax import lax

QUERIES = 128
TILE = 64
BLOCKS_DEV = 2
TILES_DEV = 256
RELATIONS = 3
HOPS = 3
ENTITIES = 32768
N_ROW = 16
N_COL = 16


def draw_tile_coords(key, part):
    key_rows, key_left, key_right, key_order = jax.random.split(key, 4)
    shape = (N_ROW, N_COL, RELATIONS, TILES_DEV)
    span_rows = N_COL * BLOCKS_DEV
    span_cols = N_ROW * BLOCKS_DEV
    row_index = jax.random.randint(key_rows, shape, 0, span_rows, dtype=jnp.int32)
    left = jax.random.randint(key_left, shape, 0, span_cols, dtype=jnp.int32)
    right = jax.random.randint(key_right, shape, 0, span_cols, dtype=jnp.int32)
    order = jax.random.permutation(key_order, span_cols).astype(jnp.int32)
    col_index = order[left * right // span_cols]
    row_index = row_index.at[..., 0].set(span_rows - 1)
    col_index = col_index.at[..., 1].set(span_cols - 1)
    return jnp.stack([row_index, col_index], axis=3).astype(jnp.int32)


def draw_tile_count(key, part):
    key_shift, key_full = jax.random.split(key, 2)
    shift = jax.random.randint(key_shift, (N_ROW * N_COL, RELATIONS), 0, 4, dtype=jnp.int32)
    counts = jnp.floor_divide(TILES_DEV, jnp.left_shift(jnp.ones_like(shift), shift))
    fullest = jax.random.randint(key_full, (RELATIONS,), 0, N_ROW * N_COL, dtype=jnp.int32)
    counts = counts.at[fullest, jnp.arange(RELATIONS)].set(TILES_DEV)
    return counts.reshape(N_ROW, N_COL, RELATIONS).astype(jnp.int32)


def plant(values, own_key, low, top_value):
    spot = [jax.random.randint(jax.random.fold_in(own_key, axis), (), 0, length) for axis, length in enumerate(values.shape)]
    main_axis = values.shape.index(max(values.shape))
    beside = spot[:main_axis] + [(spot[main_axis] + 1) % values.shape[main_axis]] + spot[main_axis + 1:]
    return values.at[tuple(spot)].set(low).at[tuple(beside)].set(top_value)


def steps_of(rng, dims, cuts, least, largest):
    factor_of, own = 1.0, jax.random.fold_in(rng, 6)
    for axis_at, parts in cuts:
        draws = jnp.exp(jax.random.uniform(jax.random.fold_in(own, axis_at), (parts,), jnp.float32, least / len(cuts), largest / len(cuts)))
        factor_of = factor_of * jnp.repeat(draws, dims[axis_at] // parts).reshape([-1 if axis == axis_at else 1 for axis in range(len(dims))])
    return factor_of


def centred(key, extent, scale, reach, pieces=(), kind=jnp.bfloat16):
    loudness = steps_of(key, extent, pieces, -0.22, 0.18) if pieces else 1.0
    drawn = jax.random.normal(key, extent, jnp.float32) * scale * loudness
    return jnp.minimum(jnp.maximum(drawn, -reach), reach).astype(kind)


def setup_inputs(seed: int = 0) -> dict:
    arg_keys = jax.random.split(jax.random.key(seed), 6)
    return {
        "tiles": centred(arg_keys[0], (N_ROW, N_COL, RELATIONS, TILES_DEV // 2, TILE, 2 * TILE), (TILE * TILES_DEV // BLOCKS_DEV) ** -0.5, 0.0625, ((0, 16), (1, 16)), jnp.float32),
        "tile_coords": draw_tile_coords(jax.random.fold_in(arg_keys[5], 71), 0),
        "tile_count": draw_tile_count(jax.random.fold_in(arg_keys[5], 71), 0),
        "seeds": plant(jax.random.randint(arg_keys[3], (QUERIES,), 0, ENTITIES), jax.random.fold_in(arg_keys[3], 1), 0, ENTITIES - 1).astype(jnp.int32),
        "chain": jax.random.randint(arg_keys[4], (HOPS,), 0, RELATIONS).astype(jnp.int32),
    }


def paired_products(pair_values, picked):
    pair_total = pair_values.shape[0]
    split_values = pair_values.reshape(pair_total, TILE, 2, TILE)
    split_states = picked.reshape(pair_total, 2, TILE, QUERIES)
    product = jnp.einsum('sahb,shbq->shaq', split_values, split_states, precision=lax.Precision.HIGHEST)
    return product.reshape(pair_total * 2, TILE, QUERIES)

def apply_relation(state, tiles, tile_coords, tile_count, relation):
    column_view = state.reshape(N_ROW, N_COL, BLOCKS_DEV * TILE, QUERIES)
    out_blocks = N_COL * BLOCKS_DEV
    zero_index = jnp.zeros((), jnp.int32)
    relation = relation.astype(jnp.int32)

    def one_row(grid_row):
        grid_row = grid_row.astype(jnp.int32)

        def one_col(total, grid_col):
            grid_col = grid_col.astype(jnp.int32)
            segment = lax.dynamic_index_in_dim(column_view, grid_col, 1, keepdims=False)
            blocks = segment.reshape(N_ROW * BLOCKS_DEV, TILE, QUERIES)
            values = lax.dynamic_slice(tiles, (grid_row, grid_col, relation, zero_index, zero_index, zero_index), (1, 1, 1, TILES_DEV // 2, TILE, 2 * TILE))[0, 0, 0]
            coords = lax.dynamic_slice(tile_coords, (grid_row, grid_col, relation, zero_index, zero_index), (1, 1, 1, 2, TILES_DEV))[0, 0, 0]
            live_count = lax.dynamic_slice(tile_count, (grid_row, grid_col, relation), (1, 1, 1))[0, 0, 0]
            picked = blocks[coords[1]]
            product = paired_products(values, picked)
            live = jnp.arange(TILES_DEV, dtype=jnp.int32) < live_count
            product = jnp.where(live[:, None, None], product, jnp.zeros_like(product))
            return (total + jax.ops.segment_sum(product, coords[0], num_segments=out_blocks), None)
        start = jnp.zeros((out_blocks, TILE, QUERIES), state.dtype)
        total, _ = lax.scan(one_col, start, jnp.arange(N_COL, dtype=jnp.int32))
        return total
    rows_out = lax.map(one_row, jnp.arange(N_ROW, dtype=jnp.int32))
    return rows_out.reshape(N_ROW * N_COL * BLOCKS_DEV * TILE, QUERIES)

def reference(tiles, tile_coords, tile_count, seeds, chain):
    entity_ids = jnp.arange(ENTITIES, dtype=jnp.int32)
    state = (entity_ids[:, None] == seeds.astype(jnp.int32)[None, :]).astype(tiles.dtype)
    for step_index in range(HOPS):
        state = apply_relation(state, tiles, tile_coords, tile_count, chain[step_index].astype(jnp.int32))
    totals = lax.optimization_barrier(jnp.sum(state * state, axis=0))
    return state * lax.rsqrt(totals / ENTITIES + 1e-06)
```

```python
import functools

import jax
import jax.numpy as jnp
from jax import lax
from jax.experimental import pallas as pl
from jax.experimental.pallas import tpu as pltpu
from jax.sharding import PartitionSpec as P

QUERIES = 128
TILE = 64
BLOCK = 128
SLOTS = 256
RELATIONS = 3
HOPS = 3
NX, NY, NZ = 4, 4, 8
NROW = NX * NY
NCOL = NZ * 2
CELLS = 2 * NCOL * NROW
ENTITIES = NROW * NCOL * BLOCK
MESH = pl.DeviceIdType.MESH
F32 = jnp.float32
BF16 = jnp.bfloat16


def merge_kernel(chain, count, coords, tiles, cells, table, slots, merged, in_sem, out_sem):
    loads = []
    for h in range(HOPS):
        copy = pltpu.make_async_copy(tiles.at[chain[h]], slots.at[h], in_sem.at[h])
        copy.start()
        loads.append(copy)
    high = lax.broadcasted_iota(jnp.int32, (TILE, 2 * TILE), 1) >= TILE
    stores = []
    for h in range(HOPS):
        m = chain[h]

        @pl.loop(0, CELLS // 16)
        def _(n):
            for k in range(16):
                table[h * CELLS + n * 16 + k] = SLOTS

        merged[h, SLOTS] = jnp.zeros((TILE, 2 * TILE), F32)
        loads[h].wait()

        @pl.loop(0, count[m] // 4)
        def _(n):
            for k in range(4):
                t = n * 4 + k
                i = coords[m, 0, t]
                j = coords[m, 1, t]
                block = ((i // 2) % 2) * 16 + (i // 4) * 2 + i % 2
                key = h * CELLS + block * NROW + j // 2
                side = j % 2
                found = table[key]
                fresh = found == SLOTS
                target = jnp.where(fresh, t, found)
                table[key] = target
                shift = jnp.where(side == k % 2, 0, TILE)
                value = pltpu.roll(slots[h, n * 2 + k // 2], shift, 1)
                value = jnp.where(high == (side == 1), value, 0.0)
                merged[h, target] = value + jnp.where(fresh, 0.0, merged[h, target])

        copy = pltpu.make_async_copy(merged.at[h], cells.at[h], out_sem.at[h])
        copy.start()
        stores.append(copy)
    for copy in stores:
        copy.wait()


def merge(chain, count, coords, tiles):
    smem = pl.BlockSpec(memory_space=pltpu.SMEM)
    anywhere = pl.BlockSpec(memory_space=pl.ANY)
    return pl.pallas_call(
        merge_kernel,
        out_shape=(
            jax.ShapeDtypeStruct((HOPS, SLOTS + 1, TILE, 2 * TILE), F32),
            jax.ShapeDtypeStruct((HOPS * CELLS,), jnp.int32),
        ),
        in_specs=[smem, smem, smem, anywhere],
        out_specs=(anywhere, smem),
        scratch_shapes=[
            pltpu.VMEM((HOPS, SLOTS // 2, TILE, 2 * TILE), F32),
            pltpu.VMEM((HOPS, SLOTS + 1, TILE, 2 * TILE), F32),
            pltpu.SemaphoreType.DMA((HOPS,)),
            pltpu.SemaphoreType.DMA((HOPS,)),
        ],
        compiler_params=pltpu.CompilerParams(vmem_limit_bytes=56 * 2**20),
        name="merge_slots",
    )(chain, count, coords, tiles)


def chain_kernel(
    table, seeds, cells, out,
    held_a, held_b, dense_hi, dense_lo, right, part, cross, ring, state, col_tot, row_tot,
    load_sem, cross_sem, ring_sem, gather_sem, tot_sem,
):
    p = lax.axis_index("row")
    q = lax.axis_index("col")
    x, y = p // NY, p % NY
    z, core = q // 2, q % 2
    other = 1 - core

    def remote(src, dst, send, recv, device):
        return pltpu.make_async_remote_copy(
            src_ref=src, dst_ref=dst, send_sem=send, recv_sem=recv, device_id=device, device_id_type=MESH
        )

    held = (held_a, held_b, held_a)

    def load(h):
        return pltpu.make_async_copy(cells.at[h], held[h], load_sem.at[h])

    load(0).start()
    load(1).start()
    barrier = pltpu.get_barrier_semaphore()

    @pl.loop(1, 16)
    def _(d):
        pl.semaphore_signal(barrier, inc=1, device_id=(p, (q + d) % NCOL), device_id_type=MESH)
        pl.semaphore_signal(barrier, inc=1, device_id=((p + d) % NROW, q), device_id_type=MESH)

    def assemble(h, start, stop):
        @pl.loop(start, stop)
        def _(block):
            rows = pl.ds(pl.multiple_of(block * TILE, TILE), TILE)
            for s in range(NROW):
                value = held[h][table[h * CELLS + block * NROW + s]]
                top = value.astype(BF16)
                dense_hi[s, rows, :] = top
                dense_lo[s, rows, :] = (value - top.astype(F32)).astype(BF16)

    def multiply(half):
        @pl.loop(0, 2)
        def _(m):
            first = half * 8 + m * 4
            rows = pl.ds(pl.multiple_of(first * BLOCK, 4 * BLOCK), 4 * BLOCK)
            left = jnp.concatenate([dense_hi[s, rows, :] for s in range(NROW)], axis=1)
            both = jnp.dot(left, right[...], preferred_element_type=F32)
            left = jnp.concatenate([dense_lo[s, rows, :] for s in range(NROW)], axis=1)
            low = jnp.dot(left, right[:, :QUERIES], preferred_element_type=F32)
            total = both[:, :QUERIES] + both[:, QUERIES:] + low
            part[pl.ds(first, 4)] = total.reshape(4, BLOCK, QUERIES)

    load(0).wait()
    assemble(0, 0, 32)
    load(2).start()
    offsets = lax.broadcasted_iota(jnp.int32, (BLOCK, QUERIES), 0)
    for s in range(NROW):
        ids = (s * NCOL + q) * BLOCK + offsets
        hit = jnp.where(ids == seeds[...], 1.0, 0.0).astype(BF16)
        right[s * BLOCK:(s + 1) * BLOCK, :QUERIES] = hit
        right[s * BLOCK:(s + 1) * BLOCK, QUERIES:] = jnp.zeros((BLOCK, QUERIES), BF16)

    for h in range(HOPS):
        sends = []
        multiply(other)
        if h == 0:
            pl.semaphore_wait(barrier, 30)

        def crossing(o):
            block = (z + o) % NZ
            return remote(
                part.at[other * 8 + block], cross.at[h, block],
                cross_sem.at[0, h, o], cross_sem.at[1, h, o], (p, z * 2 + other),
            )

        order = (4, 3, 5, 2, 6, 1, 7, 0)
        for o in order:
            copy = crossing(o)
            copy.start()
            sends.append(copy)
        multiply(core)

        def half_rows(u):
            return pl.ds(u * TILE, TILE)

        def along(way, k, u, src):
            near = (z + (1 if way == 0 else NZ - 1)) % NZ
            return remote(
                src, ring.at[h, way, k - 1, half_rows(u)],
                ring_sem.at[0, h, way, k - 1, u], ring_sem.at[1, h, way, k - 1, u], (p, near * 2 + core),
            )

        def mine(o):
            return core * 8 + (z + o) % NZ

        def start(way, k, u, src):
            copy = along(way, k, u, src)
            copy.start()
            sends.append(copy)

        for o in order:
            crossing(o).wait_recv()
            part[mine(o)] = part[mine(o)] + cross[h, (z + o) % NZ]
            if o == 4:
                start(0, 4, 0, part.at[mine(4), half_rows(0)])
                start(1, 4, 1, part.at[mine(4), half_rows(1)])
            if o == 3:
                start(0, 3, 1, part.at[mine(3), half_rows(1)])
            if o == 5:
                start(1, 3, 0, part.at[mine(5), half_rows(0)])

        def relay(way, k, u):
            slot = ring.at[h, way, k - 1, half_rows(u)]
            along(way, k, u, slot).wait_recv()
            o = k - 1 if way == 0 else NZ - (k - 1)
            slot[...] = slot[...] + part[mine(o), half_rows(u), :]
            start(way, k - 1, u, slot)

        pieces = iter(range(0, 32, 8))

        def fill():
            if h + 1 < HOPS:
                at = next(pieces)
                if at == 0:
                    load(h + 1).wait()
                assemble(h + 1, at, at + 8)

        fill()
        relay(0, 4, 0)
        relay(1, 4, 1)
        relay(0, 3, 1)
        relay(1, 3, 0)
        fill()
        relay(0, 3, 0)
        relay(1, 3, 1)
        relay(0, 2, 1)
        relay(1, 2, 0)
        fill()
        relay(0, 2, 0)
        relay(1, 2, 1)

        def finished(u):
            for way in range(2):
                along(way, 1, u, ring.at[h, way, 0, half_rows(u)]).wait_recv()
            return part[mine(0), half_rows(u), :] + ring[h, 0, 0, half_rows(u), :] + ring[h, 1, 0, half_rows(u), :]

        if h + 1 < HOPS:
            used = [0, 0]

            def spread(u, source, device):
                copy = remote(
                    state.at[h, source, half_rows(u)], state.at[h, source, half_rows(u)],
                    gather_sem.at[0, h, u, used[u]], gather_sem.at[1, h, u, source], device,
                )
                used[u] += 1
                copy.start()
                sends.append(copy)

            def across(u, d):
                return ((x + d) % NX) * NY + y if u == 0 else x * NY + (y + d) % NY

            def arrived(u, source):
                remote(
                    state.at[h, source, half_rows(u)], state.at[h, source, half_rows(u)],
                    gather_sem.at[0, h, u, 0], gather_sem.at[1, h, u, source], (p, z * 2 + other),
                ).wait_recv()

            for u in range(2):
                state[h, p, half_rows(u), :] = finished(u)
                for d in (2, 1, 3):
                    spread(u, p, (across(u, d), q))
                for d in (2, 1, 3):
                    spread(u, p, (across(1 - u, d), q))
            fill()
            for d in (1, 3, 2):
                for u in range(2):
                    source = across(u, d)
                    arrived(u, source)
                    for e in (2, 1, 3):
                        spot = (x * NY + (y + e) % NY if u == 0 else ((x + e) % NX) * NY + y, q)
                        spread(u, source, spot)
            for u in range(2):
                for d in range(NX):
                    for e in (1, 2, 3):
                        if u == 0:
                            arrived(u, ((x + d) % NX) * NY + (y + e) % NY)
                        else:
                            arrived(u, ((x + e) % NX) * NY + (y + d) % NY)
            for s in range(NROW):
                value = state[h, s]
                top = value.astype(BF16)
                right[s * BLOCK:(s + 1) * BLOCK, :QUERIES] = top
                right[s * BLOCK:(s + 1) * BLOCK, QUERIES:] = (value - top.astype(F32)).astype(BF16)
        else:
            for u in range(2):
                out[half_rows(u), :] = finished(u)
        for copy in sends:
            copy.wait_send()

    owned = out[...]
    col_tot[q] = jnp.sum((owned * owned).reshape(16, 8, QUERIES), axis=0)

    def total(d, stage):
        if stage == 0:
            return remote(col_tot.at[q], col_tot.at[q], tot_sem.at[0, 0, d], tot_sem.at[1, 0, d], (p, (q + d) % NCOL))
        return remote(row_tot.at[p], row_tot.at[p], tot_sem.at[0, 1, d], tot_sem.at[1, 1, d], ((p + d) % NROW, q))

    for stage in range(2):
        @pl.loop(1, 16)
        def _(d):
            total(d, stage).start()

        @pl.loop(1, 16)
        def _(d):
            total(d, stage).wait()

        if stage == 0:
            row_tot[p] = jnp.sum(col_tot[...], axis=0)
    totals = jnp.sum(jnp.sum(row_tot[...], axis=0), axis=0, keepdims=True)
    out[...] = owned * lax.rsqrt(totals / ENTITIES + 1e-06)


def run_chain(table, seeds, cells):
    smem = pl.BlockSpec(memory_space=pltpu.SMEM)
    vmem = pl.BlockSpec(memory_space=pltpu.VMEM)
    anywhere = pl.BlockSpec(memory_space=pl.ANY)
    return pl.pallas_call(
        chain_kernel,
        out_shape=jax.ShapeDtypeStruct((BLOCK, QUERIES), F32),
        in_specs=[smem, vmem, anywhere],
        out_specs=vmem,
        scratch_shapes=[
            pltpu.VMEM((SLOTS + 1, TILE, 2 * TILE), F32),
            pltpu.VMEM((SLOTS + 1, TILE, 2 * TILE), F32),
            pltpu.VMEM((NROW, NCOL * BLOCK, BLOCK), BF16),
            pltpu.VMEM((NROW, NCOL * BLOCK, BLOCK), BF16),
            pltpu.VMEM((NROW * BLOCK, 2 * QUERIES), BF16),
            pltpu.VMEM((NCOL, BLOCK, QUERIES), F32),
            pltpu.VMEM((HOPS, NZ, BLOCK, QUERIES), F32),
            pltpu.VMEM((HOPS, 2, 4, BLOCK, QUERIES), F32),
            pltpu.VMEM((HOPS - 1, NROW, BLOCK, QUERIES), F32),
            pltpu.VMEM((NCOL, 8, QUERIES), F32),
            pltpu.VMEM((NROW, 8, QUERIES), F32),
            pltpu.SemaphoreType.DMA((HOPS,)),
            pltpu.SemaphoreType.DMA((2, HOPS, NZ)),
            pltpu.SemaphoreType.DMA((2, HOPS, 2, 4, 2)),
            pltpu.SemaphoreType.DMA((2, HOPS - 1, 2, 16)),
            pltpu.SemaphoreType.DMA((2, 2, 16)),
        ],
        compiler_params=pltpu.CompilerParams(
            collective_id=0, has_side_effects=True, vmem_limit_bytes=56 * 2**20
        ),
        name="relation_chain",
    )(table, seeds, cells)


def shards(tiles, tile_coords, tile_count, seeds, chain):
    cells, table = merge(chain, tile_count[0, 0], tile_coords[0, 0], tiles[0, 0])
    return run_chain(table, seeds.reshape(1, QUERIES), cells)


def solution(mesh):
    in_specs = (
        P("row", "col", None, None, None, None),
        P("row", "col", None, None, None),
        P("row", "col", None),
        P(),
        P(),
    )
    out_specs = P(("row", "col"), None)
    return jax.shard_map(shards, mesh=mesh, in_specs=in_specs, out_specs=out_specs, check_vma=False)
```

```python
import jax
import jax.numpy as jnp
from jax import lax
from jax.experimental import pallas as pl
from jax.experimental.pallas import tpu as pltpu
from jax.sharding import PartitionSpec as P

QUERIES = 128
TILE = 64
BLOCK = 128
SLOTS = 256
HOPS = 3
NX, NY, NZ = 4, 4, 8
NROW = NX * NY
NCOL = NZ * 2
CELLS = 2 * NCOL * NROW
ENTITIES = NROW * NCOL * BLOCK
MESH = pl.DeviceIdType.MESH
F32 = jnp.float32
BF16 = jnp.bfloat16


def merge_kernel(
    chain, count, coords, seeds, tiles, cells, plan, product, slots, merged, rows, seed_rows, in_sem, out_sem, plan_sem
):
    order = (1, 2, 0)
    loads = {}
    for h in order:
        loads[h] = pltpu.make_async_copy(tiles.at[chain[h]], slots.at[h], in_sem.at[h])
        loads[h].start()
    lane = lax.broadcasted_iota(jnp.int32, (SLOTS, SLOTS), 1)
    line = lax.broadcasted_iota(jnp.int32, (SLOTS, SLOTS), 0)
    slot = lax.broadcasted_iota(jnp.int32, (1, SLOTS), 1)
    for h in range(HOPS):
        pair = coords[chain[h]]
        i, j = pair[0:1, :], pair[1:2, :]
        block = ((i >> 1) & 1) * 16 + (i >> 2) * 2 + (i & 1)
        if h == 0:
            word = block + (j << 8)
        else:
            key = jnp.where(slot < count[chain[h]], block * NROW + (j >> 1), CELLS + slot)
            keys = jnp.sum(jnp.where(lane == line, key, 0), axis=1, keepdims=True)
            first = jnp.min(jnp.where(keys == key, line, SLOTS), axis=0, keepdims=True)
            word = first + (jnp.where(first == slot, SLOTS, first) << 9) + ((j & 1) << 18)
            for n in range(CELLS // 128):
                cell = lane[:, :128] + n * 128
                found = jnp.where(keys == cell, line[:, :128], SLOTS)
                rows[h * 8 + n:h * 8 + n + 1, :] = jnp.min(found, axis=0, keepdims=True)
        for n in range(SLOTS // 128):
            rows[h * 8 + 4 + n:h * 8 + 5 + n, :] = word[:, n * 128:(n + 1) * 128]
    copy = pltpu.make_async_copy(rows, plan, plan_sem)
    copy.start()
    q = lax.axis_index("col")
    offsets = lax.broadcasted_iota(jnp.int32, (TILE, QUERIES), 0)
    for j in range(2 * NROW):
        ids = ((j // 2) * NCOL + q) * BLOCK + (j % 2) * TILE + offsets
        seed_rows[j] = jnp.where(ids == seeds[...], 1.0, 0.0).astype(BF16)
    product[...] = jnp.zeros_like(product)
    copy.wait()
    side_of = lax.broadcasted_iota(jnp.int32, (TILE, 2 * TILE), 1) >> 6
    stores = []
    for h in (1, 2):
        merged[h - 1, SLOTS] = jnp.zeros((TILE, 2 * TILE), F32)
        loads[h].wait()

        @pl.loop(0, count[chain[h]] // 32)
        def _(n):
            for u in range(16):
                value = slots[h, n * 16 + u]
                swapped = pltpu.roll(value, TILE, 1)
                for k in range(2):
                    t = n * 32 + u * 2 + k
                    word = plan[h * 8 + 4 + (t >> 7), t & 127]
                    side = word >> 18
                    base = merged[h - 1, (word >> 9) & 511]
                    moved = jnp.where(side == k, value, swapped)
                    merged[h - 1, word & 511] = base + jnp.where(side_of == side, moved, 0.0)

        copy = pltpu.make_async_copy(merged.at[h - 1], cells.at[h - 1], out_sem.at[h - 1])
        copy.start()
        stores.append(copy)
    loads[0].wait()
    none = jnp.zeros((TILE, QUERIES), BF16)

    @pl.loop(0, count[chain[0]] // 16)
    def _(n):
        for u in range(8):
            value = slots[0, n * 8 + u]
            top = value.astype(BF16)
            low = (value - top.astype(F32)).astype(BF16)
            t = n * 16 + u * 2
            words = [plan[4 + ((t + k) >> 7), (t + k) & 127] for k in range(2)]
            left = jnp.concatenate([seed_rows[words[0] >> 8], none], axis=0)
            right = jnp.concatenate([none, seed_rows[words[1] >> 8]], axis=0)
            both = jnp.dot(
                jnp.concatenate([top, low], axis=0), jnp.concatenate([left, right], axis=1), preferred_element_type=F32
            )
            both = both[:TILE] + both[TILE:]
            for k in range(2):
                at = words[k] & 255
                product[at] = product[at] + both[:, k * QUERIES:(k + 1) * QUERIES]

    for copy in stores:
        copy.wait()


def merge(chain, count, coords, seeds, tiles):
    smem = pl.BlockSpec(memory_space=pltpu.SMEM)
    vmem = pl.BlockSpec(memory_space=pltpu.VMEM)
    anywhere = pl.BlockSpec(memory_space=pl.ANY)
    return pl.pallas_call(
        merge_kernel,
        out_shape=(
            jax.ShapeDtypeStruct((HOPS - 1, SLOTS + 1, TILE, 2 * TILE), F32),
            jax.ShapeDtypeStruct((HOPS * 8, 128), jnp.int32),
            jax.ShapeDtypeStruct((2 * NCOL, TILE, QUERIES), F32),
        ),
        in_specs=[smem, smem, vmem, vmem, anywhere],
        out_specs=(anywhere, smem, vmem),
        scratch_shapes=[
            pltpu.VMEM((HOPS, SLOTS // 2, TILE, 2 * TILE), F32),
            pltpu.VMEM((HOPS - 1, SLOTS + 1, TILE, 2 * TILE), F32),
            pltpu.VMEM((HOPS * 8, 128), jnp.int32),
            pltpu.VMEM((2 * NROW, TILE, QUERIES), BF16),
            pltpu.SemaphoreType.DMA((HOPS,)),
            pltpu.SemaphoreType.DMA((HOPS - 1,)),
            pltpu.SemaphoreType.DMA,
        ],
        compiler_params=pltpu.CompilerParams(vmem_limit_bytes=48 * 2**20),
        name="first_hop_and_cells",
    )(chain, count, coords, seeds, tiles)


def chain_kernel(
    table, first, cells, out,
    held_a, held_b, dense_hi, dense_lo, right, part, cross, ring, state, col_tot, row_tot,
    load_sem, cross_sem, ring_sem, gather_sem, tot_sem,
):
    p = lax.axis_index("row")
    q = lax.axis_index("col")
    x, y = p // NY, p % NY
    z, core = q // 2, q % 2
    other = 1 - core
    held = (None, held_a, held_b)

    def remote(src, dst, send, recv, device):
        return pltpu.make_async_remote_copy(
            src_ref=src, dst_ref=dst, send_sem=send, recv_sem=recv, device_id=device, device_id_type=MESH
        )

    def load(h):
        return pltpu.make_async_copy(cells.at[h - 1], held[h], load_sem.at[h - 1])

    barrier = pltpu.get_barrier_semaphore()

    @pl.loop(1, 16)
    def _(d):
        pl.semaphore_signal(barrier, inc=1, device_id=(p, (q + d) % NCOL), device_id_type=MESH)
        pl.semaphore_signal(barrier, inc=1, device_id=((p + d) % NROW, q), device_id_type=MESH)

    load(1).start()
    load(2).start()

    def assemble(h, start, stop):
        @pl.loop(start, stop)
        def _(block):
            rows = pl.ds(pl.multiple_of(block * TILE, TILE), TILE)
            for s in range(NROW):
                value = held[h][table[h * 8 + (block >> 3), (block & 7) * NROW + s]]
                top = value.astype(BF16)
                dense_hi[s, rows, :] = top
                dense_lo[s, rows, :] = (value - top.astype(F32)).astype(BF16)

    def split(h, gx):
        for k in range(NY):
            value = state[h - 1, gx * NY + k]
            top = value.astype(BF16)
            right[k * BLOCK:(k + 1) * BLOCK, :QUERIES] = top
            right[k * BLOCK:(k + 1) * BLOCK, QUERIES:] = (value - top.astype(F32)).astype(BF16)

    def multiply(gx, half, fresh):
        @pl.loop(0, 2)
        def _(m):
            at = half * 8 + m * 4
            rows = pl.ds(pl.multiple_of(at * BLOCK, 4 * BLOCK), 4 * BLOCK)
            left = jnp.concatenate([dense_hi[gx * NY + k, rows, :] for k in range(NY)], axis=1)
            both = jnp.dot(left, right[...], preferred_element_type=F32)
            left = jnp.concatenate([dense_lo[gx * NY + k, rows, :] for k in range(NY)], axis=1)
            low = jnp.dot(left, right[:, :QUERIES], preferred_element_type=F32)
            total = (both[:, :QUERIES] + both[:, QUERIES:] + low).reshape(4, BLOCK, QUERIES)
            part[pl.ds(at, 4)] = total if fresh else part[pl.ds(at, 4)] + total

    def half_rows(u):
        return pl.ds(u * TILE, TILE)

    def away(way, k):
        return (z + (k if way == 0 else NZ - k)) % NZ

    pl.semaphore_wait(barrier, 30)
    sends = []

    def go(copy):
        copy.start()
        sends.append(copy)

    def block_at(h, u, source):
        return state.at[h, source, half_rows(u)]

    def across(u, d):
        return ((x + d) % NX) * NY + y if u == 0 else x * NY + (y + d) % NY

    def arrived(h, u, source):
        remote(
            block_at(h, u, source), block_at(h, u, source),
            gather_sem.at[0, h, u, 0], gather_sem.at[1, h, u, source], (p, z * 2 + other),
        ).wait_recv()

    for h in range(HOPS):
        whole = first if h == 0 else part

        def crossing(o):
            block = (z + o) % NZ
            return remote(
                whole.at[other * 8 + block], cross.at[h, block],
                cross_sem.at[0, h, o], cross_sem.at[1, h, o], (p, z * 2 + other),
            )

        order = (4, 3, 5, 1, 7, 2, 6, 0)
        if h > 0:
            groups = (0, 1, 3, 2)
            for n, d in enumerate(groups):
                gx = (x + d) % NX
                for u in range(2):
                    for e in range(NY):
                        if (e if u == 0 else d) != 0:
                            arrived(h - 1, u, gx * NY + (y + e) % NY)
                split(h, gx)
                multiply(gx, other, n == 0)
                if n == NX - 1:
                    for o in order:
                        copy = crossing(o)
                        copy.start()
                        crossed.append(copy)
                multiply(gx, core, n == 0)
        else:
            crossed = []
            for o in order:
                copy = crossing(o)
                copy.start()
                crossed.append(copy)

        def sum_of(o):
            return cross.at[h, (z + o) % NZ]

        def along(way, n, u, src, k):
            return remote(
                src, ring.at[h, way, n, half_rows(u)],
                ring_sem.at[0, h, way, n, u], ring_sem.at[1, h, way, n, u], (p, away(way, k) * 2 + core),
            )

        def got(way, n, u):
            along(way, n, u, ring.at[h, way, n, half_rows(u)], 1).wait_recv()

        for o in order:
            crossing(o).wait_recv()
            block = (z + o) % NZ
            cross[h, block] = cross[h, block] + whole[core * 8 + block]
            if o == 4:
                go(along(0, 3, 0, sum_of(4).at[half_rows(0)], 2))
                go(along(1, 3, 1, sum_of(4).at[half_rows(1)], 2))
            elif o in (3, 5):
                for u in range(2):
                    go(along(o // 4, 2, u, sum_of(o).at[half_rows(u)], 1))
            elif o in (1, 7):
                for u in range(2):
                    go(along(o // 4, 0, u, sum_of(o).at[half_rows(u)], 1))
        if h + 1 < HOPS:
            load(h + 1).wait()
            assemble(h + 1, 0, 16)
        for u in range(2):
            for way in range(2):
                got(way, 2, u)
                total = ring[h, way, 2, half_rows(u), :] + cross[h, away(way, 2), half_rows(u), :]
                if u == way:
                    got(way, 3, u)
                    total = total + ring[h, way, 3, half_rows(u), :]
                ring[h, way, 2, half_rows(u), :] = total
                go(along(way, 1, u, ring.at[h, way, 2, half_rows(u)], 2))
        if h + 1 < HOPS:
            assemble(h + 1, 16, 32)

        def finished(u):
            total = cross[h, z, half_rows(u), :]
            for n in (0, 1):
                for way in range(2):
                    got(way, n, u)
                    total = total + ring[h, way, n, half_rows(u), :]
            return total

        for copy in crossed:
            copy.wait_send()
        crossed = []
        if h + 1 < HOPS:
            used = [0, 0]

            def spread(u, source, device):
                go(remote(
                    block_at(h, u, source), block_at(h, u, source),
                    gather_sem.at[0, h, u, used[u]], gather_sem.at[1, h, u, source], device,
                ))
                used[u] += 1

            for u in range(2):
                state[h, p, half_rows(u), :] = finished(u)
                for d in (2, 1, 3):
                    spread(u, p, (across(u, d), q))
                for d in (2, 1, 3):
                    spread(u, p, (across(1 - u, d), q))
            for d in (1, 3, 2):
                for u in range(2):
                    arrived(h, u, across(u, d))
                    for e in (2, 1, 3):
                        spread(u, across(u, d), (x * NY + (y + e) % NY if u == 0 else ((x + e) % NX) * NY + y, q))
        else:
            for u in range(2):
                out[half_rows(u), :] = finished(u)

    owned = out[...]
    col_tot[q] = jnp.sum((owned * owned).reshape(16, 8, QUERIES), axis=0)

    def total(d, stage):
        if stage == 0:
            return remote(col_tot.at[q], col_tot.at[q], tot_sem.at[0, 0, d], tot_sem.at[1, 0, d], (p, (q + d) % NCOL))
        return remote(row_tot.at[p], row_tot.at[p], tot_sem.at[0, 1, d], tot_sem.at[1, 1, d], ((p + d) % NROW, q))

    for stage in range(2):
        @pl.loop(1, 16)
        def _(d):
            total(d, stage).start()

        @pl.loop(1, 16)
        def _(d):
            total(d, stage).wait()

        if stage == 0:
            row_tot[p] = jnp.sum(col_tot[...], axis=0)
    totals = jnp.sum(jnp.sum(row_tot[...], axis=0), axis=0, keepdims=True)
    out[...] = owned * lax.rsqrt(totals / ENTITIES + 1e-06)
    for copy in sends:
        copy.wait_send()


def run_chain(table, first, cells):
    smem = pl.BlockSpec(memory_space=pltpu.SMEM)
    vmem = pl.BlockSpec(memory_space=pltpu.VMEM)
    anywhere = pl.BlockSpec(memory_space=pl.ANY)
    return pl.pallas_call(
        chain_kernel,
        out_shape=jax.ShapeDtypeStruct((BLOCK, QUERIES), F32),
        in_specs=[smem, vmem, anywhere],
        out_specs=vmem,
        scratch_shapes=[
            pltpu.VMEM((SLOTS + 1, TILE, 2 * TILE), F32),
            pltpu.VMEM((SLOTS + 1, TILE, 2 * TILE), F32),
            pltpu.VMEM((NROW, NCOL * BLOCK, BLOCK), BF16),
            pltpu.VMEM((NROW, NCOL * BLOCK, BLOCK), BF16),
            pltpu.VMEM((NY * BLOCK, 2 * QUERIES), BF16),
            pltpu.VMEM((NCOL, BLOCK, QUERIES), F32),
            pltpu.VMEM((HOPS, NZ, BLOCK, QUERIES), F32),
            pltpu.VMEM((HOPS, 2, 4, BLOCK, QUERIES), F32),
            pltpu.VMEM((HOPS - 1, NROW, BLOCK, QUERIES), F32),
            pltpu.VMEM((NCOL, 8, QUERIES), F32),
            pltpu.VMEM((NROW, 8, QUERIES), F32),
            pltpu.SemaphoreType.DMA((HOPS - 1,)),
            pltpu.SemaphoreType.DMA((2, HOPS, NZ)),
            pltpu.SemaphoreType.DMA((2, HOPS, 2, 4, 2)),
            pltpu.SemaphoreType.DMA((2, HOPS - 1, 2, 16)),
            pltpu.SemaphoreType.DMA((2, 2, 16)),
        ],
        compiler_params=pltpu.CompilerParams(
            collective_id=0, has_side_effects=True, vmem_limit_bytes=54 * 2**20
        ),
        name="relation_chain",
    )(table, first, cells)


def shards(tiles, tile_coords, tile_count, seeds, chain):
    cells, table, product = merge(
        chain, tile_count[0, 0], tile_coords[0, 0], seeds.reshape(1, QUERIES), tiles[0, 0]
    )
    return run_chain(table, product.reshape(NCOL, BLOCK, QUERIES), cells)


def solution(mesh):
    in_specs = (
        P("row", "col", None, None, None, None),
        P("row", "col", None, None, None),
        P("row", "col", None),
        P(),
        P(),
    )
    out_specs = P(("row", "col"), None)
    return jax.shard_map(shards, mesh=mesh, in_specs=in_specs, out_specs=out_specs, check_vma=False)
```

```python
import jax
import jax.numpy as jnp
from jax import lax
from jax.experimental import pallas as pl
from jax.experimental.pallas import tpu as pltpu
from jax.sharding import PartitionSpec as P

QUERIES = 128
TILE = 64
BLOCK = 128
SLOTS = 256
HOPS = 3
NX, NY, NZ = 4, 4, 8
NROW = NX * NY
NCOL = NZ * 2
CELLS = 2 * NCOL * NROW
ENTITIES = NROW * NCOL * BLOCK
MESH = pl.DeviceIdType.MESH
F32 = jnp.float32
BF16 = jnp.bfloat16


def merge_kernel(
    chain_hbm, count_hbm, coords_hbm, seeds_hbm, tiles, cells, plan_hbm, product_hbm,
    chain, count, coords, seeds, plan, product, slots, merged, rows, seed_rows, small_sem, in_sem, out_sem, plan_sem,
):
    pairs = ((chain_hbm, chain), (count_hbm, count), (coords_hbm, coords), (seeds_hbm, seeds))
    small = [pltpu.make_async_copy(src, dst, small_sem.at[n]) for n, (src, dst) in enumerate(pairs)]
    for copy in small:
        copy.start()
    product[...] = jnp.zeros_like(product)
    small[0].wait()
    order = (1, 2, 0)
    loads = {}
    for h in order:
        loads[h] = pltpu.make_async_copy(tiles.at[chain[h]], slots.at[h], in_sem.at[h])
        loads[h].start()
    for copy in small[1:]:
        copy.wait()
    lane = lax.broadcasted_iota(jnp.int32, (SLOTS, SLOTS), 1)
    line = lax.broadcasted_iota(jnp.int32, (SLOTS, SLOTS), 0)
    slot = lax.broadcasted_iota(jnp.int32, (1, SLOTS), 1)
    for h in range(HOPS):
        pair = coords[chain[h]]
        i, j = pair[0:1, :], pair[1:2, :]
        block = ((i >> 1) & 1) * 16 + (i >> 2) * 2 + (i & 1)
        if h == 0:
            word = block + (j << 8)
        else:
            key = jnp.where(slot < count[chain[h]], block * NROW + (j >> 1), CELLS + slot)
            keys = jnp.sum(jnp.where(lane == line, key, 0), axis=1, keepdims=True)
            first = jnp.min(jnp.where(keys == key, line, SLOTS), axis=0, keepdims=True)
            word = first + (jnp.where(first == slot, SLOTS, first) << 9) + ((j & 1) << 18)
            for n in range(CELLS // 128):
                cell = lane[:, :128] + n * 128
                found = jnp.where(keys == cell, line[:, :128], SLOTS)
                rows[h * 8 + n:h * 8 + n + 1, :] = jnp.min(found, axis=0, keepdims=True)
        for n in range(SLOTS // 128):
            rows[h * 8 + 4 + n:h * 8 + 5 + n, :] = word[:, n * 128:(n + 1) * 128]
    copy = pltpu.make_async_copy(rows, plan, plan_sem.at[0])
    copy.start()
    stores = [pltpu.make_async_copy(rows, plan_hbm, plan_sem.at[1])]
    stores[0].start()
    q = lax.axis_index("col")
    offsets = lax.broadcasted_iota(jnp.int32, (TILE, QUERIES), 0)
    for j in range(2 * NROW):
        ids = ((j // 2) * NCOL + q) * BLOCK + (j % 2) * TILE + offsets
        seed_rows[j] = jnp.where(ids == seeds[...], 1.0, 0.0).astype(BF16)
    copy.wait()
    side_of = lax.broadcasted_iota(jnp.int32, (TILE, 2 * TILE), 1) >> 6
    for h in (1, 2):
        merged[h - 1, SLOTS] = jnp.zeros((TILE, 2 * TILE), F32)
        loads[h].wait()

        @pl.loop(0, count[chain[h]] // 32)
        def _(n):
            for u in range(16):
                value = slots[h, n * 16 + u]
                swapped = pltpu.roll(value, TILE, 1)
                for k in range(2):
                    t = n * 32 + u * 2 + k
                    word = plan[h * 8 + 4 + (t >> 7), t & 127]
                    side = word >> 18
                    base = merged[h - 1, (word >> 9) & 511]
                    moved = jnp.where(side == k, value, swapped)
                    merged[h - 1, word & 511] = base + jnp.where(side_of == side, moved, 0.0)

        copy = pltpu.make_async_copy(merged.at[h - 1], cells.at[h - 1], out_sem.at[h - 1])
        copy.start()
        stores.append(copy)
    loads[0].wait()
    none = jnp.zeros((TILE, QUERIES), BF16)

    @pl.loop(0, count[chain[0]] // 16)
    def _(n):
        for u in range(8):
            value = slots[0, n * 8 + u]
            top = value.astype(BF16)
            low = (value - top.astype(F32)).astype(BF16)
            t = n * 16 + u * 2
            words = [plan[4 + ((t + k) >> 7), (t + k) & 127] for k in range(2)]
            left = jnp.concatenate([seed_rows[words[0] >> 8], none], axis=0)
            right = jnp.concatenate([none, seed_rows[words[1] >> 8]], axis=0)
            both = jnp.dot(
                jnp.concatenate([top, low], axis=0), jnp.concatenate([left, right], axis=1), preferred_element_type=F32
            )
            both = both[:TILE] + both[TILE:]
            for k in range(2):
                at = words[k] & 255
                product[at] = product[at] + both[:, k * QUERIES:(k + 1) * QUERIES]

    copy = pltpu.make_async_copy(product, product_hbm, plan_sem.at[2])
    copy.start()
    stores.append(copy)
    for copy in stores:
        copy.wait()


def merge(chain, count, coords, seeds, tiles):
    hbm = pl.BlockSpec(memory_space=pltpu.HBM)
    return pl.pallas_call(
        merge_kernel,
        out_shape=(
            jax.ShapeDtypeStruct((HOPS - 1, SLOTS + 1, TILE, 2 * TILE), F32),
            jax.ShapeDtypeStruct((HOPS * 8, 128), jnp.int32),
            jax.ShapeDtypeStruct((2 * NCOL, TILE, QUERIES), F32),
        ),
        in_specs=[hbm] * 5,
        out_specs=(hbm, hbm, hbm),
        scratch_shapes=[
            pltpu.SMEM((HOPS,), jnp.int32),
            pltpu.SMEM((HOPS,), jnp.int32),
            pltpu.VMEM((HOPS, 2, SLOTS), jnp.int32),
            pltpu.VMEM((1, QUERIES), jnp.int32),
            pltpu.SMEM((HOPS * 8, 128), jnp.int32),
            pltpu.VMEM((2 * NCOL, TILE, QUERIES), F32),
            pltpu.VMEM((HOPS, SLOTS // 2, TILE, 2 * TILE), F32),
            pltpu.VMEM((HOPS - 1, SLOTS + 1, TILE, 2 * TILE), F32),
            pltpu.VMEM((HOPS * 8, 128), jnp.int32),
            pltpu.VMEM((2 * NROW, TILE, QUERIES), BF16),
            pltpu.SemaphoreType.DMA((4,)),
            pltpu.SemaphoreType.DMA((HOPS,)),
            pltpu.SemaphoreType.DMA((HOPS - 1,)),
            pltpu.SemaphoreType.DMA((3,)),
        ],
        compiler_params=pltpu.CompilerParams(vmem_limit_bytes=60 * 2**20),
        name="first_hop_and_cells",
    )(chain, count, coords, seeds, tiles)


def chain_kernel(
    table_hbm, first, cells, out,
    table, held_a, held_b, dense_hi, dense_lo, right, part, cross, ring, state, col_tot, row_tot,
    load_sem, sent_sem, cross_sem, ring_sem, gather_sem, tot_sem,
):
    p = lax.axis_index("row")
    q = lax.axis_index("col")
    x, y = p // NY, p % NY
    z, core = q // 2, q % 2
    other = 1 - core
    held = (None, held_a, held_b)

    def remote(src, dst, send, recv, device):
        return pltpu.make_async_remote_copy(
            src_ref=src, dst_ref=dst, send_sem=send, recv_sem=recv, device_id=device, device_id_type=MESH
        )

    def load(h):
        return pltpu.make_async_copy(cells.at[h - 1], held[h], load_sem.at[h - 1])

    barrier = pltpu.get_barrier_semaphore()

    @pl.loop(1, 16)
    def _(d):
        pl.semaphore_signal(barrier, inc=1, device_id=(p, (q + d) % NCOL), device_id_type=MESH)
        pl.semaphore_signal(barrier, inc=1, device_id=((p + d) % NROW, q), device_id_type=MESH)

    fetches = [
        pltpu.make_async_copy(first, part, load_sem.at[2]), pltpu.make_async_copy(table_hbm, table, load_sem.at[3]),
    ]
    for copy in fetches:
        copy.start()
    load(1).start()
    load(2).start()

    def assemble(h, start, stop):
        @pl.loop(start, stop)
        def _(block):
            rows = pl.ds(pl.multiple_of(block * TILE, TILE), TILE)
            for s in range(NROW):
                value = held[h][table[h * 8 + (block >> 3), (block & 7) * NROW + s]]
                top = value.astype(BF16)
                dense_hi[s, rows, :] = top
                dense_lo[s, rows, :] = (value - top.astype(F32)).astype(BF16)

    def split(h, gx):
        for k in range(NY):
            value = state[h - 1, gx * NY + k]
            top = value.astype(BF16)
            right[k * BLOCK:(k + 1) * BLOCK, :QUERIES] = top
            right[k * BLOCK:(k + 1) * BLOCK, QUERIES:] = (value - top.astype(F32)).astype(BF16)

    def multiply(gx, half, fresh):
        @pl.loop(0, 2)
        def _(m):
            at = half * 8 + m * 4
            rows = pl.ds(pl.multiple_of(at * BLOCK, 4 * BLOCK), 4 * BLOCK)
            left = jnp.concatenate([dense_hi[gx * NY + k, rows, :] for k in range(NY)], axis=1)
            both = jnp.dot(left, right[...], preferred_element_type=F32)
            left = jnp.concatenate([dense_lo[gx * NY + k, rows, :] for k in range(NY)], axis=1)
            low = jnp.dot(left, right[:, :QUERIES], preferred_element_type=F32)
            total = (both[:, :QUERIES] + both[:, QUERIES:] + low).reshape(4, BLOCK, QUERIES)
            part[pl.ds(at, 4)] = total if fresh else part[pl.ds(at, 4)] + total

    def half_rows(u):
        return pl.ds(u * TILE, TILE)

    def away(way, k):
        return (z + (k if way == 0 else NZ - k)) % NZ

    for copy in fetches:
        copy.wait()
    pl.semaphore_wait(barrier, 30)

    def sent(kind, h, ref):
        remote(ref, ref, sent_sem.at[kind, h], sent_sem.at[kind, h], (p, z * 2 + other)).wait_send()

    def block_at(h, u, source):
        return state.at[h, source, half_rows(u)]

    def across(u, d):
        return ((x + d) % NX) * NY + y if u == 0 else x * NY + (y + d) % NY

    def arrived(h, u, source):
        remote(
            block_at(h, u, source), block_at(h, u, source),
            sent_sem.at[1, h], gather_sem.at[h, u, source], (p, z * 2 + other),
        ).wait_recv()

    for h in range(HOPS):

        def crossing(o):
            block = (z + o) % NZ
            return remote(
                part.at[other * 8 + block], cross.at[h, block],
                sent_sem.at[0, h], cross_sem.at[h, o], (p, z * 2 + other),
            )

        order = (4, 3, 5, 1, 7, 2, 6, 0)
        if h > 0:
            groups = (0, 1, 3, 2)
            for n, d in enumerate(groups):
                gx = (x + d) % NX
                for u in range(2):
                    for e in range(NY):
                        if (e if u == 0 else d) != 0:
                            arrived(h - 1, u, gx * NY + (y + e) % NY)
                split(h, gx)
                multiply(gx, other, n == 0)
                if n == NX - 1:
                    for o in order:
                        crossing(o).start()
                multiply(gx, core, n == 0)
        else:
            for o in order:
                crossing(o).start()

        def sum_of(o):
            return cross.at[h, (z + o) % NZ]

        def along(way, n, u, src, k):
            return remote(
                src, ring.at[h, way, n, half_rows(u)],
                sent_sem.at[2, h], ring_sem.at[h, way, n, u], (p, away(way, k) * 2 + core),
            )

        def got(way, n, u):
            along(way, n, u, ring.at[h, way, n, half_rows(u)], 1).wait_recv()

        for o in order:
            crossing(o).wait_recv()
            block = (z + o) % NZ
            cross[h, block] = cross[h, block] + part[core * 8 + block]
            if o == 4:
                along(0, 3, 0, sum_of(4).at[half_rows(0)], 2).start()
                along(1, 3, 1, sum_of(4).at[half_rows(1)], 2).start()
            elif o in (3, 5):
                for u in range(2):
                    along(o // 4, 2, u, sum_of(o).at[half_rows(u)], 1).start()
            elif o in (1, 7):
                for u in range(2):
                    along(o // 4, 0, u, sum_of(o).at[half_rows(u)], 1).start()
        if h + 1 < HOPS:
            load(h + 1).wait()
            assemble(h + 1, 0, 16)
        for u in range(2):
            for way in range(2):
                got(way, 2, u)
                total = ring[h, way, 2, half_rows(u), :] + cross[h, away(way, 2), half_rows(u), :]
                if u == way:
                    got(way, 3, u)
                    total = total + ring[h, way, 3, half_rows(u), :]
                ring[h, way, 2, half_rows(u), :] = total
                along(way, 1, u, ring.at[h, way, 2, half_rows(u)], 2).start()
        if h + 1 < HOPS:
            assemble(h + 1, 16, 32)

        def finished(u):
            total = cross[h, z, half_rows(u), :]
            for n in (0, 1):
                for way in range(2):
                    got(way, n, u)
                    total = total + ring[h, way, n, half_rows(u), :]
            return total

        sent(0, h, part.at[pl.ds(0, NZ)])
        if h + 1 < HOPS:
            def spread(u, source, device):
                remote(
                    block_at(h, u, source), block_at(h, u, source),
                    sent_sem.at[1, h], gather_sem.at[h, u, source], device,
                ).start()

            for u in range(2):
                state[h, p, half_rows(u), :] = finished(u)
                for d in (2, 1, 3):
                    spread(u, p, (across(u, d), q))
                for d in (2, 1, 3):
                    spread(u, p, (across(1 - u, d), q))
            for d in (1, 3, 2):
                for u in range(2):
                    arrived(h, u, across(u, d))
                    for e in (2, 1, 3):
                        spread(u, across(u, d), (x * NY + (y + e) % NY if u == 0 else ((x + e) % NX) * NY + y, q))
        else:
            for u in range(2):
                out[half_rows(u), :] = finished(u)

    owned = out[...]
    col_tot[q] = jnp.sum((owned * owned).reshape(16, 8, QUERIES), axis=0)

    far_first = (8, 7, 9, 6, 10, 5, 11, 4, 12, 3, 13, 2, 14, 1, 15)
    for stage, (tot, me) in enumerate(((col_tot, q), (row_tot, p))):
        for d in far_first:
            device = (p, (q + d) % NCOL) if stage == 0 else ((p + d) % NROW, q)
            remote(tot.at[me], tot.at[me], tot_sem.at[0, stage], tot_sem.at[1, stage], device).start()
        every = tot.at[pl.ds(0, 15)]
        remote(every, every, tot_sem.at[0, stage], tot_sem.at[1, stage], (p, z * 2 + other)).wait()
        if stage == 0:
            row_tot[p] = jnp.sum(col_tot[...], axis=0)
    totals = jnp.sum(jnp.sum(row_tot[...], axis=0), axis=0, keepdims=True)
    out[...] = owned * lax.rsqrt(totals / ENTITIES + 1e-06)
    for h in range(HOPS):
        sent(2, h, cross.at[0, pl.ds(0, 7)])
    for h in range(HOPS - 1):
        sent(1, h, state.at[0, pl.ds(0, NROW - 1)])


def run_chain(table, first, cells):
    vmem = pl.BlockSpec(memory_space=pltpu.VMEM)
    hbm = pl.BlockSpec(memory_space=pltpu.HBM)
    return pl.pallas_call(
        chain_kernel,
        out_shape=jax.ShapeDtypeStruct((BLOCK, QUERIES), F32),
        in_specs=[hbm] * 3,
        out_specs=vmem,
        scratch_shapes=[
            pltpu.SMEM((HOPS * 8, 128), jnp.int32),
            pltpu.VMEM((SLOTS + 1, TILE, 2 * TILE), F32),
            pltpu.VMEM((SLOTS + 1, TILE, 2 * TILE), F32),
            pltpu.VMEM((NROW, NCOL * BLOCK, BLOCK), BF16),
            pltpu.VMEM((NROW, NCOL * BLOCK, BLOCK), BF16),
            pltpu.VMEM((NY * BLOCK, 2 * QUERIES), BF16),
            pltpu.VMEM((NCOL, BLOCK, QUERIES), F32),
            pltpu.VMEM((HOPS, NZ, BLOCK, QUERIES), F32),
            pltpu.VMEM((HOPS, 2, 4, BLOCK, QUERIES), F32),
            pltpu.VMEM((HOPS - 1, NROW, BLOCK, QUERIES), F32),
            pltpu.VMEM((NCOL, 8, QUERIES), F32),
            pltpu.VMEM((NROW, 8, QUERIES), F32),
            pltpu.SemaphoreType.DMA((4,)),
            pltpu.SemaphoreType.DMA((3, HOPS)),
            pltpu.SemaphoreType.DMA((HOPS, NZ)),
            pltpu.SemaphoreType.DMA((HOPS, 2, 4, 2)),
            pltpu.SemaphoreType.DMA((HOPS - 1, 2, 16)),
            pltpu.SemaphoreType.DMA((2, 2)),
        ],
        compiler_params=pltpu.CompilerParams(
            collective_id=0, has_side_effects=True, vmem_limit_bytes=60 * 2**20
        ),
        name="relation_chain",
    )(table, first, cells)


def shards(tiles, tile_coords, tile_count, seeds, chain):
    cells, table, product = merge(
        chain, tile_count[0, 0], tile_coords[0, 0], seeds.reshape(1, QUERIES), tiles[0, 0]
    )
    return run_chain(table, product.reshape(NCOL, BLOCK, QUERIES), cells)


def solution(mesh):
    in_specs = (
        P("row", "col", None, None, None, None),
        P("row", "col", None, None, None),
        P("row", "col", None),
        P(),
        P(),
    )
    out_specs = P(("row", "col"), None)
    return jax.shard_map(shards, mesh=mesh, in_specs=in_specs, out_specs=out_specs, check_vma=False)
```

```python
import jax
import jax.numpy as jnp
from jax import lax
from jax.experimental import pallas as pl
from jax.experimental.pallas import tpu as pltpu
from jax.sharding import PartitionSpec as P

QUERIES = 128
TILE = 64
BLOCK = 128
SLOTS = 256
HOPS = 3
NX, NY, NZ = 4, 4, 8
NROW = NX * NY
NCOL = NZ * 2
CELLS = 2 * NCOL * NROW
ENTITIES = NROW * NCOL * BLOCK
MESH = pl.DeviceIdType.MESH
F32 = jnp.float32
BF16 = jnp.bfloat16


def merge_kernel(
    chain_hbm, count_hbm, coords_hbm, seeds_hbm, tiles, cells, plan_hbm, product_hbm,
    chain, count, coords, seeds, plan, product, slots, merged, rows, seed_rows, small_sem, in_sem, out_sem, plan_sem,
):
    pairs = ((chain_hbm, chain), (count_hbm, count), (coords_hbm, coords), (seeds_hbm, seeds))
    small = [pltpu.make_async_copy(src, dst, small_sem.at[n]) for n, (src, dst) in enumerate(pairs)]
    for copy in small:
        copy.start()
    product[...] = jnp.zeros_like(product)
    small[0].wait()
    order = (1, 2, 0)
    loads = {}
    for h in order:
        loads[h] = pltpu.make_async_copy(tiles.at[chain[h]], slots.at[h], in_sem.at[h])
        loads[h].start()
    for copy in small[1:]:
        copy.wait()
    lane = lax.broadcasted_iota(jnp.int32, (SLOTS, SLOTS), 1)
    line = lax.broadcasted_iota(jnp.int32, (SLOTS, SLOTS), 0)
    slot = lax.broadcasted_iota(jnp.int32, (1, SLOTS), 1)
    for h in range(HOPS):
        pair = coords[chain[h]]
        i, j = pair[0:1, :], pair[1:2, :]
        block = ((i >> 1) & 1) * 16 + (i >> 2) * 2 + (i & 1)
        if h == 0:
            word = block + (j << 8)
        else:
            along_x, along_y = j >> 3, (j >> 1) & 3
            second = (j & 1) == 1
            couple = jnp.where(second, 8 + along_y * 2 + (along_x >> 1), along_x * 2 + (along_y >> 1))
            side = jnp.where(second, along_x & 1, along_y & 1)
            key = jnp.where(slot < count[chain[h]], block * NROW + couple, CELLS + slot)
            keys = jnp.sum(jnp.where(lane == line, key, 0), axis=1, keepdims=True)
            first = jnp.min(jnp.where(keys == key, line, SLOTS), axis=0, keepdims=True)
            word = first + (jnp.where(first == slot, SLOTS, first) << 9) + (side << 18)
            for n in range(CELLS // 128):
                cell = lane[:, :128] + n * 128
                found = jnp.where(keys == cell, line[:, :128], SLOTS)
                rows[h * 8 + n:h * 8 + n + 1, :] = jnp.min(found, axis=0, keepdims=True)
        for n in range(SLOTS // 128):
            rows[h * 8 + 4 + n:h * 8 + 5 + n, :] = word[:, n * 128:(n + 1) * 128]
    copy = pltpu.make_async_copy(rows, plan, plan_sem.at[0])
    copy.start()
    stores = [pltpu.make_async_copy(rows, plan_hbm, plan_sem.at[1])]
    stores[0].start()
    q = lax.axis_index("col")
    offsets = lax.broadcasted_iota(jnp.int32, (TILE, QUERIES), 0)
    for j in range(2 * NROW):
        ids = ((j // 2) * NCOL + q) * BLOCK + (j % 2) * TILE + offsets
        seed_rows[j] = jnp.where(ids == seeds[...], 1.0, 0.0).astype(BF16)
    copy.wait()
    side_of = lax.broadcasted_iota(jnp.int32, (TILE, 2 * TILE), 1) >> 6
    for h in (1, 2):
        merged[h - 1, SLOTS] = jnp.zeros((TILE, 2 * TILE), F32)
        loads[h].wait()

        @pl.loop(0, count[chain[h]] // 32)
        def _(n):
            for u in range(16):
                value = slots[h, n * 16 + u]
                swapped = pltpu.roll(value, TILE, 1)
                for k in range(2):
                    t = n * 32 + u * 2 + k
                    word = plan[h * 8 + 4 + (t >> 7), t & 127]
                    side = word >> 18
                    base = merged[h - 1, (word >> 9) & 511]
                    moved = jnp.where(side == k, value, swapped)
                    merged[h - 1, word & 511] = base + jnp.where(side_of == side, moved, 0.0)

        copy = pltpu.make_async_copy(merged.at[h - 1], cells.at[h - 1], out_sem.at[h - 1])
        copy.start()
        stores.append(copy)
    loads[0].wait()
    none = jnp.zeros((TILE, QUERIES), BF16)

    @pl.loop(0, count[chain[0]] // 16)
    def _(n):
        for u in range(8):
            value = slots[0, n * 8 + u]
            top = value.astype(BF16)
            low = (value - top.astype(F32)).astype(BF16)
            t = n * 16 + u * 2
            words = [plan[4 + ((t + k) >> 7), (t + k) & 127] for k in range(2)]
            left = jnp.concatenate([seed_rows[words[0] >> 8], none], axis=0)
            right = jnp.concatenate([none, seed_rows[words[1] >> 8]], axis=0)
            both = jnp.dot(
                jnp.concatenate([top, low], axis=0), jnp.concatenate([left, right], axis=1), preferred_element_type=F32
            )
            both = both[:TILE] + both[TILE:]
            for k in range(2):
                at = words[k] & 255
                product[at] = product[at] + both[:, k * QUERIES:(k + 1) * QUERIES]

    copy = pltpu.make_async_copy(product, product_hbm, plan_sem.at[2])
    copy.start()
    stores.append(copy)
    for copy in stores:
        copy.wait()


def merge(chain, count, coords, seeds, tiles):
    hbm = pl.BlockSpec(memory_space=pltpu.HBM)
    return pl.pallas_call(
        merge_kernel,
        out_shape=(
            jax.ShapeDtypeStruct((HOPS - 1, SLOTS + 1, TILE, 2 * TILE), F32),
            jax.ShapeDtypeStruct((HOPS * 8, 128), jnp.int32),
            jax.ShapeDtypeStruct((2 * NCOL, TILE, QUERIES), F32),
        ),
        in_specs=[hbm] * 5,
        out_specs=(hbm, hbm, hbm),
        scratch_shapes=[
            pltpu.SMEM((HOPS,), jnp.int32),
            pltpu.SMEM((HOPS,), jnp.int32),
            pltpu.VMEM((HOPS, 2, SLOTS), jnp.int32),
            pltpu.VMEM((1, QUERIES), jnp.int32),
            pltpu.SMEM((HOPS * 8, 128), jnp.int32),
            pltpu.VMEM((2 * NCOL, TILE, QUERIES), F32),
            pltpu.VMEM((HOPS, SLOTS // 2, TILE, 2 * TILE), F32),
            pltpu.VMEM((HOPS - 1, SLOTS + 1, TILE, 2 * TILE), F32),
            pltpu.VMEM((HOPS * 8, 128), jnp.int32),
            pltpu.VMEM((2 * NROW, TILE, QUERIES), BF16),
            pltpu.SemaphoreType.DMA((4,)),
            pltpu.SemaphoreType.DMA((HOPS,)),
            pltpu.SemaphoreType.DMA((HOPS - 1,)),
            pltpu.SemaphoreType.DMA((3,)),
        ],
        compiler_params=pltpu.CompilerParams(vmem_limit_bytes=60 * 2**20),
        name="first_hop_and_cells",
    )(chain, count, coords, seeds, tiles)


def chain_kernel(
    table_hbm, first, cells, out,
    table, held_a, held_b, dense_hi, dense_lo, right, part, cross, ring, state, col_tot, row_tot,
    load_sem, sent_sem, cross_sem, ring_sem, gather_sem, tot_sem,
):
    p = lax.axis_index("row")
    q = lax.axis_index("col")
    x, y = p // NY, p % NY
    z, core = q // 2, q % 2
    other = 1 - core
    held = (None, held_a, held_b)

    def remote(src, dst, send, recv, device):
        return pltpu.make_async_remote_copy(
            src_ref=src, dst_ref=dst, send_sem=send, recv_sem=recv, device_id=device, device_id_type=MESH
        )

    def load(h):
        return pltpu.make_async_copy(cells.at[h - 1], held[h], load_sem.at[h - 1])

    barrier = pltpu.get_barrier_semaphore()

    @pl.loop(1, 16)
    def _(d):
        pl.semaphore_signal(barrier, inc=1, device_id=(p, (q + d) % NCOL), device_id_type=MESH)
        pl.semaphore_signal(barrier, inc=1, device_id=((p + d) % NROW, q), device_id_type=MESH)

    fetches = [
        pltpu.make_async_copy(first, part, load_sem.at[2]), pltpu.make_async_copy(table_hbm, table, load_sem.at[3]),
    ]
    for copy in fetches:
        copy.start()
    load(1).start()
    load(2).start()

    def assemble(h, start, stop):
        @pl.loop(start, stop)
        def _(block):
            rows = pl.ds(pl.multiple_of(block * TILE, TILE), TILE)
            for s in range(NROW):
                value = held[h][table[h * 8 + (block >> 3), (block & 7) * NROW + s]]
                top = value.astype(BF16)
                dense_hi[s, rows, :] = top
                dense_lo[s, rows, :] = (value - top.astype(F32)).astype(BF16)

    def split(h, d):
        gx, gy = (x + d) % NX, (y + d) % NY
        for u in range(2):
            for k in range(NX):
                value = state[h - 1, gx * NY + k if u == 0 else k * NY + gy, u * TILE:(u + 1) * TILE, :]
                top = value.astype(BF16)
                at = (u * NX + k) * TILE
                right[at:at + TILE, :QUERIES] = top
                right[at:at + TILE, QUERIES:] = (value - top.astype(F32)).astype(BF16)

    def multiply(d, start, steps):
        gx, gy = (x + d) % NX, (y + d) % NY
        couples = (gx * 2, gx * 2 + 1, 8 + gy * 2, 9 + gy * 2)

        @pl.loop(0, steps)
        def _(m):
            at = start + m * 8
            rows = pl.ds(pl.multiple_of(at * BLOCK, 8 * BLOCK), 8 * BLOCK)
            left = jnp.concatenate([dense_hi[c, rows, :] for c in couples], axis=1)
            both = jnp.dot(left, right[...], preferred_element_type=F32)
            left = jnp.concatenate([dense_lo[c, rows, :] for c in couples], axis=1)
            low = jnp.dot(left, right[:, :QUERIES], preferred_element_type=F32)
            total = both[:, :QUERIES] + both[:, QUERIES:] + low
            part[pl.ds(at, 8)] = part[pl.ds(at, 8)] + total.reshape(8, BLOCK, QUERIES)

    def half_rows(u):
        return pl.ds(u * TILE, TILE)

    def away(way, k):
        return (z + (k if way == 0 else NZ - k)) % NZ

    for copy in fetches:
        copy.wait()
    pl.semaphore_wait(barrier, 30)

    def sent(kind, h, ref):
        remote(ref, ref, sent_sem.at[kind, h], sent_sem.at[kind, h], (p, z * 2 + other)).wait_send()

    def block_at(h, u, source):
        return state.at[h, source, half_rows(u)]

    def across(u, d):
        return ((x + d) % NX) * NY + y if u == 0 else x * NY + (y + d) % NY

    def arrived(h, u, source):
        remote(
            block_at(h, u, source), block_at(h, u, source),
            sent_sem.at[1, h], gather_sem.at[h, u, source], (p, z * 2 + other),
        ).wait_recv()

    for h in range(HOPS):

        def crossing(o):
            block = (z + o) % NZ
            return remote(
                part.at[other * 8 + block], cross.at[h, block],
                sent_sem.at[0, h], cross_sem.at[h, o], (p, z * 2 + other),
            )

        order = (4, 3, 5, 1, 7, 2, 6, 0)
        if h > 0:
            def columns(d):
                for e in (1, 2, 3):
                    arrived(h - 1, 0, ((x + d) % NX) * NY + (y + e) % NY)
                    arrived(h - 1, 1, ((x + e) % NX) * NY + (y + d) % NY)
                split(h, d)

            part[...] = jnp.zeros_like(part)

            @pl.loop(0, NX - 1)
            def _(n):
                columns(n + n // 2)
                multiply(n + n // 2, 0, 2)

            columns(2)
            multiply(2, other * 8, 1)
            for o in order:
                crossing(o).start()
            multiply(2, core * 8, 1)
        else:
            for o in order:
                crossing(o).start()

        def sum_of(o):
            return cross.at[h, (z + o) % NZ]

        def along(way, n, u, src, k):
            return remote(
                src, ring.at[h, way, n, half_rows(u)],
                sent_sem.at[2, h], ring_sem.at[h, way, n, u], (p, away(way, k) * 2 + core),
            )

        def got(way, n, u):
            along(way, n, u, ring.at[h, way, n, half_rows(u)], 1).wait_recv()

        for o in order:
            crossing(o).wait_recv()
            block = (z + o) % NZ
            cross[h, block] = cross[h, block] + part[core * 8 + block]
            if o == 4:
                along(0, 3, 0, sum_of(4).at[half_rows(0)], 2).start()
                along(1, 3, 1, sum_of(4).at[half_rows(1)], 2).start()
            elif o in (3, 5):
                for u in range(2):
                    along(o // 4, 2, u, sum_of(o).at[half_rows(u)], 1).start()
            elif o in (1, 7):
                for u in range(2):
                    along(o // 4, 0, u, sum_of(o).at[half_rows(u)], 1).start()
        if h + 1 < HOPS:
            load(h + 1).wait()
            assemble(h + 1, 0, 16)
        for u in range(2):
            for way in range(2):
                got(way, 2, u)
                total = ring[h, way, 2, half_rows(u), :] + cross[h, away(way, 2), half_rows(u), :]
                if u == way:
                    got(way, 3, u)
                    total = total + ring[h, way, 3, half_rows(u), :]
                ring[h, way, 2, half_rows(u), :] = total
                along(way, 1, u, ring.at[h, way, 2, half_rows(u)], 2).start()
        if h + 1 < HOPS:
            assemble(h + 1, 16, 32)

        def finished(u):
            total = cross[h, z, half_rows(u), :]
            for n in (0, 1):
                for way in range(2):
                    got(way, n, u)
                    total = total + ring[h, way, n, half_rows(u), :]
            return total

        sent(0, h, part.at[pl.ds(0, NZ)])
        if h + 1 < HOPS:
            def spread(u, source, device):
                remote(
                    block_at(h, u, source), block_at(h, u, source),
                    sent_sem.at[1, h], gather_sem.at[h, u, source], device,
                ).start()

            for u in range(2):
                state[h, p, half_rows(u), :] = finished(u)
                for d in (1, 3, 2):
                    spread(u, p, (across(u, d), q))
                for d in (1, 3, 2):
                    spread(u, p, (across(1 - u, d), q))
            for d in (1, 3, 2):
                for u in range(2):
                    arrived(h, u, across(u, d))
                    for e in (1, 3, 2):
                        spread(u, across(u, d), (x * NY + (y + e) % NY if u == 0 else ((x + e) % NX) * NY + y, q))
        else:
            for u in range(2):
                out[half_rows(u), :] = finished(u)

    owned = out[...]
    col_tot[q] = jnp.sum((owned * owned).reshape(16, 8, QUERIES), axis=0)

    far_first = (8, 7, 9, 6, 10, 5, 11, 4, 12, 3, 13, 2, 14, 1, 15)
    for stage, (tot, me) in enumerate(((col_tot, q), (row_tot, p))):
        for d in far_first:
            device = (p, (q + d) % NCOL) if stage == 0 else ((p + d) % NROW, q)
            remote(tot.at[me], tot.at[me], tot_sem.at[0, stage], tot_sem.at[1, stage], device).start()
        every = tot.at[pl.ds(0, 15)]
        remote(every, every, tot_sem.at[0, stage], tot_sem.at[1, stage], (p, z * 2 + other)).wait()
        if stage == 0:
            row_tot[p] = jnp.sum(col_tot[...], axis=0)
    totals = jnp.sum(jnp.sum(row_tot[...], axis=0), axis=0, keepdims=True)
    out[...] = owned * lax.rsqrt(totals / ENTITIES + 1e-06)
    for h in range(HOPS):
        sent(2, h, cross.at[0, pl.ds(0, 7)])
    for h in range(HOPS - 1):
        sent(1, h, state.at[0, pl.ds(0, NROW - 1)])


def run_chain(table, first, cells):
    vmem = pl.BlockSpec(memory_space=pltpu.VMEM)
    hbm = pl.BlockSpec(memory_space=pltpu.HBM)
    return pl.pallas_call(
        chain_kernel,
        out_shape=jax.ShapeDtypeStruct((BLOCK, QUERIES), F32),
        in_specs=[hbm] * 3,
        out_specs=vmem,
        scratch_shapes=[
            pltpu.SMEM((HOPS * 8, 128), jnp.int32),
            pltpu.VMEM((SLOTS + 1, TILE, 2 * TILE), F32),
            pltpu.VMEM((SLOTS + 1, TILE, 2 * TILE), F32),
            pltpu.VMEM((NROW, NCOL * BLOCK, BLOCK), BF16),
            pltpu.VMEM((NROW, NCOL * BLOCK, BLOCK), BF16),
            pltpu.VMEM((NY * BLOCK, 2 * QUERIES), BF16),
            pltpu.VMEM((NCOL, BLOCK, QUERIES), F32),
            pltpu.VMEM((HOPS, NZ, BLOCK, QUERIES), F32),
            pltpu.VMEM((HOPS, 2, 4, BLOCK, QUERIES), F32),
            pltpu.VMEM((HOPS - 1, NROW, BLOCK, QUERIES), F32),
            pltpu.VMEM((NCOL, 8, QUERIES), F32),
            pltpu.VMEM((NROW, 8, QUERIES), F32),
            pltpu.SemaphoreType.DMA((4,)),
            pltpu.SemaphoreType.DMA((3, HOPS)),
            pltpu.SemaphoreType.DMA((HOPS, NZ)),
            pltpu.SemaphoreType.DMA((HOPS, 2, 4, 2)),
            pltpu.SemaphoreType.DMA((HOPS - 1, 2, 16)),
            pltpu.SemaphoreType.DMA((2, 2)),
        ],
        compiler_params=pltpu.CompilerParams(
            collective_id=0, has_side_effects=True, vmem_limit_bytes=60 * 2**20
        ),
        name="relation_chain",
    )(table, first, cells)


def shards(tiles, tile_coords, tile_count, seeds, chain):
    cells, table, product = merge(
        chain, tile_count[0, 0], tile_coords[0, 0], seeds.reshape(1, QUERIES), tiles[0, 0]
    )
    return run_chain(table, product.reshape(NCOL, BLOCK, QUERIES), cells)


def solution(mesh):
    in_specs = (
        P("row", "col", None, None, None, None),
        P("row", "col", None, None, None),
        P("row", "col", None),
        P(),
        P(),
    )
    out_specs = P(("row", "col"), None)
    return jax.shard_map(shards, mesh=mesh, in_specs=in_specs, out_specs=out_specs, check_vma=False)
```

```python
import jax
import jax.numpy as jnp
from jax import lax
from jax.experimental import pallas as pl
from jax.experimental.pallas import tpu as pltpu
from jax.sharding import PartitionSpec as P

QUERIES = 128
TILE = 64
BLOCK = 128
SLOTS = 256
HOPS = 3
NX, NY, NZ = 4, 4, 8
NROW = NX * NY
NCOL = NZ * 2
CELLS = 2 * NCOL * NROW
ENTITIES = NROW * NCOL * BLOCK
MESH = pl.DeviceIdType.MESH
F32 = jnp.float32
BF16 = jnp.bfloat16


def merge_kernel(
    chain_hbm, count_hbm, coords_hbm, seeds_hbm, tiles, cells, plan_hbm, product_hbm,
    chain, count, coords, seeds, plan, product, slots, merged, rows, seed_rows, small_sem, in_sem, out_sem, plan_sem,
):
    pairs = ((chain_hbm, chain), (count_hbm, count), (coords_hbm, coords), (seeds_hbm, seeds))
    small = [pltpu.make_async_copy(src, dst, small_sem.at[n]) for n, (src, dst) in enumerate(pairs)]
    for copy in small:
        copy.start()
    product[...] = jnp.zeros_like(product)
    small[0].wait()
    order = (1, 2, 0)
    loads = {}
    for h in order:
        loads[h] = pltpu.make_async_copy(tiles.at[chain[h]], slots.at[h], in_sem.at[h])
        loads[h].start()
    for copy in small[1:]:
        copy.wait()
    lane = lax.broadcasted_iota(jnp.int32, (SLOTS, SLOTS), 1)
    line = lax.broadcasted_iota(jnp.int32, (SLOTS, SLOTS), 0)
    slot = lax.broadcasted_iota(jnp.int32, (1, SLOTS), 1)
    for h in range(HOPS):
        pair = coords[chain[h]]
        i, j = pair[0:1, :], pair[1:2, :]
        block = ((i >> 1) & 1) * 16 + (i >> 2) * 2 + (i & 1)
        if h == 0:
            word = block + (j << 8)
        else:
            along_x, along_y = j >> 3, (j >> 1) & 3
            second = (j & 1) == 1
            couple = jnp.where(second, 8 + along_y * 2 + (along_x >> 1), along_x * 2 + (along_y >> 1))
            side = jnp.where(second, along_x & 1, along_y & 1)
            key = jnp.where(slot < count[chain[h]], block * NROW + couple, CELLS + slot)
            keys = jnp.sum(jnp.where(lane == line, key, 0), axis=1, keepdims=True)
            first = jnp.min(jnp.where(keys == key, line, SLOTS), axis=0, keepdims=True)
            word = first + (jnp.where(first == slot, SLOTS, first) << 9) + (side << 18)
            for n in range(CELLS // 128):
                cell = lane[:, :128] + n * 128
                found = jnp.where(keys == cell, line[:, :128], SLOTS)
                rows[h * 8 + n:h * 8 + n + 1, :] = jnp.min(found, axis=0, keepdims=True)
        for n in range(SLOTS // 128):
            rows[h * 8 + 4 + n:h * 8 + 5 + n, :] = word[:, n * 128:(n + 1) * 128]
    copy = pltpu.make_async_copy(rows, plan, plan_sem.at[0])
    copy.start()
    stores = [pltpu.make_async_copy(rows, plan_hbm, plan_sem.at[1])]
    stores[0].start()
    q = lax.axis_index("col")
    offsets = lax.broadcasted_iota(jnp.int32, (TILE, QUERIES), 0)
    for j in range(2 * NROW):
        ids = ((j // 2) * NCOL + q) * BLOCK + (j % 2) * TILE + offsets
        seed_rows[j] = jnp.where(ids == seeds[...], 1.0, 0.0).astype(BF16)
    copy.wait()
    side_of = lax.broadcasted_iota(jnp.int32, (TILE, 2 * TILE), 1) >> 6
    for h in (1, 2):
        merged[h - 1, SLOTS] = jnp.zeros((TILE, 2 * TILE), F32)
        loads[h].wait()

        @pl.loop(0, count[chain[h]] // 32)
        def _(n):
            for u in range(16):
                value = slots[h, n * 16 + u]
                swapped = pltpu.roll(value, TILE, 1)
                for k in range(2):
                    t = n * 32 + u * 2 + k
                    word = plan[h * 8 + 4 + (t >> 7), t & 127]
                    side = word >> 18
                    base = merged[h - 1, (word >> 9) & 511]
                    moved = jnp.where(side == k, value, swapped)
                    merged[h - 1, word & 511] = base + jnp.where(side_of == side, moved, 0.0)

        copy = pltpu.make_async_copy(merged.at[h - 1], cells.at[h - 1], out_sem.at[h - 1])
        copy.start()
        stores.append(copy)
    loads[0].wait()
    none = jnp.zeros((TILE, QUERIES), BF16)

    @pl.loop(0, count[chain[0]] // 32)
    def _(n):
        for u in range(16):
            value = slots[0, n * 16 + u]
            top = value.astype(BF16)
            low = (value - top.astype(F32)).astype(BF16)
            t = n * 32 + u * 2
            words = [plan[4 + ((t + k) >> 7), (t + k) & 127] for k in range(2)]
            left = jnp.concatenate([seed_rows[words[0] >> 8], none], axis=0)
            right = jnp.concatenate([none, seed_rows[words[1] >> 8]], axis=0)
            both = jnp.dot(
                jnp.concatenate([top, low], axis=0), jnp.concatenate([left, right], axis=1), preferred_element_type=F32
            )
            both = both[:TILE] + both[TILE:]
            for k in range(2):
                at = words[k] & 255
                product[at] = product[at] + both[:, k * QUERIES:(k + 1) * QUERIES]

    copy = pltpu.make_async_copy(product, product_hbm, plan_sem.at[2])
    copy.start()
    stores.append(copy)
    for copy in stores:
        copy.wait()


def merge(chain, count, coords, seeds, tiles):
    hbm = pl.BlockSpec(memory_space=pltpu.HBM)
    return pl.pallas_call(
        merge_kernel,
        out_shape=(
            jax.ShapeDtypeStruct((HOPS - 1, SLOTS + 1, TILE, 2 * TILE), F32),
            jax.ShapeDtypeStruct((HOPS * 8, 128), jnp.int32),
            jax.ShapeDtypeStruct((2 * NCOL, TILE, QUERIES), F32),
        ),
        in_specs=[hbm] * 5,
        out_specs=(hbm, hbm, hbm),
        scratch_shapes=[
            pltpu.SMEM((HOPS,), jnp.int32),
            pltpu.SMEM((HOPS,), jnp.int32),
            pltpu.VMEM((HOPS, 2, SLOTS), jnp.int32),
            pltpu.VMEM((1, QUERIES), jnp.int32),
            pltpu.SMEM((HOPS * 8, 128), jnp.int32),
            pltpu.VMEM((2 * NCOL, TILE, QUERIES), F32),
            pltpu.VMEM((HOPS, SLOTS // 2, TILE, 2 * TILE), F32),
            pltpu.VMEM((HOPS - 1, SLOTS + 1, TILE, 2 * TILE), F32),
            pltpu.VMEM((HOPS * 8, 128), jnp.int32),
            pltpu.VMEM((2 * NROW, TILE, QUERIES), BF16),
            pltpu.SemaphoreType.DMA((4,)),
            pltpu.SemaphoreType.DMA((HOPS,)),
            pltpu.SemaphoreType.DMA((HOPS - 1,)),
            pltpu.SemaphoreType.DMA((3,)),
        ],
        compiler_params=pltpu.CompilerParams(vmem_limit_bytes=60 * 2**20),
        name="first_hop_and_cells",
    )(chain, count, coords, seeds, tiles)


def chain_kernel(
    table_hbm, first, cells, out,
    table, held_a, held_b, dense_hi, dense_lo, right, part, cross, ring, state, col_tot, row_tot,
    load_sem, sent_sem, cross_sem, ring_sem, first_sem, group_sem, tot_sem,
):
    p = lax.axis_index("row")
    q = lax.axis_index("col")
    x, y = p // NY, p % NY
    z, core = q // 2, q % 2
    other = 1 - core
    held = (None, held_a, held_b)

    def remote(src, dst, send, recv, device):
        return pltpu.make_async_remote_copy(
            src_ref=src, dst_ref=dst, send_sem=send, recv_sem=recv, device_id=device, device_id_type=MESH
        )

    def load(h):
        return pltpu.make_async_copy(cells.at[h - 1], held[h], load_sem.at[h - 1])

    barrier = pltpu.get_barrier_semaphore()

    @pl.loop(1, 16)
    def _(d):
        pl.semaphore_signal(barrier, inc=1, device_id=(p, (q + d) % NCOL), device_id_type=MESH)
        pl.semaphore_signal(barrier, inc=1, device_id=((p + d) % NROW, q), device_id_type=MESH)

    fetches = [
        pltpu.make_async_copy(first, part, load_sem.at[2]), pltpu.make_async_copy(table_hbm, table, load_sem.at[3]),
    ]
    for copy in fetches:
        copy.start()
    load(1).start()
    load(2).start()

    def assemble(h, start, stop):
        @pl.loop(start, stop)
        def _(block):
            rows = pl.ds(pl.multiple_of(block * TILE, TILE), TILE)
            for s in range(NROW):
                value = held[h][table[h * 8 + (block >> 3), (block & 7) * NROW + s]]
                top = value.astype(BF16)
                dense_hi[s, rows, :] = top
                dense_lo[s, rows, :] = (value - top.astype(F32)).astype(BF16)

    def split(h, d):
        gx, gy = (x + d) % NX, (y + d) % NY
        for u in range(2):
            for k in range(NX):
                value = state[h - 1, gx * NY + k if u == 0 else k * NY + gy, u * TILE:(u + 1) * TILE, :]
                top = value.astype(BF16)
                at = (u * NX + k) * TILE
                right[at:at + TILE, :QUERIES] = top
                right[at:at + TILE, QUERIES:] = (value - top.astype(F32)).astype(BF16)

    def multiply(d, start, steps):
        gx, gy = (x + d) % NX, (y + d) % NY
        couples = (gx * 2, gx * 2 + 1, 8 + gy * 2, 9 + gy * 2)

        @pl.loop(0, steps)
        def _(m):
            at = start + m * 8
            rows = pl.ds(pl.multiple_of(at * BLOCK, 8 * BLOCK), 8 * BLOCK)
            left = jnp.concatenate([dense_hi[c, rows, :] for c in couples], axis=1)
            both = jnp.dot(left, right[...], preferred_element_type=F32)
            left = jnp.concatenate([dense_lo[c, rows, :] for c in couples], axis=1)
            low = jnp.dot(left, right[:, :QUERIES], preferred_element_type=F32)
            total = both[:, :QUERIES] + both[:, QUERIES:] + low
            part[pl.ds(at, 8)] = part[pl.ds(at, 8)] + total.reshape(8, BLOCK, QUERIES)

    def half_rows(u):
        return pl.ds(u * TILE, TILE)

    def away(way, k):
        return (z + (k if way == 0 else NZ - k)) % NZ

    for copy in fetches:
        copy.wait()
    pl.semaphore_wait(barrier, 30)

    def sent(kind, h, ref):
        remote(ref, ref, sent_sem.at[kind, h], sent_sem.at[kind, h], (p, z * 2 + other)).wait_send()

    def block_at(h, u, source):
        return state.at[h, source, half_rows(u)]

    def across(u, d):
        return ((x + d) % NX) * NY + y if u == 0 else x * NY + (y + d) % NY

    def arrived(h, u, d):
        source = block_at(h, u, across(u, d))
        remote(source, source, sent_sem.at[1, h], first_sem.at[h, u, d - 1], (p, z * 2 + other)).wait_recv()

    def group_arrived(h, d):
        six = state.at[h, pl.ds(0, 3)]
        remote(six, six, sent_sem.at[1, h], group_sem.at[h, d], (p, z * 2 + other)).wait_recv()

    for h in range(HOPS):

        def crossing(o):
            block = (z + o) % NZ
            return remote(
                part.at[other * 8 + block], cross.at[h, block],
                sent_sem.at[0, h], cross_sem.at[h, o], (p, z * 2 + other),
            )

        order = (4, 3, 5, 1, 7, 2, 6, 0)
        if h > 0:
            def columns(d):
                group_arrived(h - 1, d)
                split(h, d)

            part[...] = jnp.zeros_like(part)

            @pl.loop(0, NX - 1)
            def _(n):
                columns(n + n // 2)
                multiply(n + n // 2, 0, 2)

            columns(2)
            multiply(2, other * 8, 1)
            for o in order:
                crossing(o).start()
            multiply(2, core * 8, 1)
        else:
            for o in order:
                crossing(o).start()

        def sum_of(o):
            return cross.at[h, (z + o) % NZ]

        def along(way, n, u, src, k):
            return remote(
                src, ring.at[h, way, n, half_rows(u)],
                sent_sem.at[2, h], ring_sem.at[h, way, n, u], (p, away(way, k) * 2 + core),
            )

        def got(way, n, u):
            along(way, n, u, ring.at[h, way, n, half_rows(u)], 1).wait_recv()

        for o in order:
            crossing(o).wait_recv()
            block = (z + o) % NZ
            cross[h, block] = cross[h, block] + part[core * 8 + block]
            if o == 4:
                along(0, 3, 0, sum_of(4).at[half_rows(0)], 2).start()
                along(1, 3, 1, sum_of(4).at[half_rows(1)], 2).start()
            elif o in (3, 5):
                for u in range(2):
                    along(o // 4, 2, u, sum_of(o).at[half_rows(u)], 1).start()
            elif o in (1, 7):
                for u in range(2):
                    along(o // 4, 0, u, sum_of(o).at[half_rows(u)], 1).start()
        if h + 1 < HOPS:
            load(h + 1).wait()
            assemble(h + 1, 0, 16)
        for u in range(2):
            for way in range(2):
                got(way, 2, u)
                total = ring[h, way, 2, half_rows(u), :] + cross[h, away(way, 2), half_rows(u), :]
                if u == way:
                    got(way, 3, u)
                    total = total + ring[h, way, 3, half_rows(u), :]
                ring[h, way, 2, half_rows(u), :] = total
                along(way, 1, u, ring.at[h, way, 2, half_rows(u)], 2).start()
        if h + 1 < HOPS:
            assemble(h + 1, 16, 32)

        def finished(u):
            total = cross[h, z, half_rows(u), :]
            for n in (0, 1):
                for way in range(2):
                    got(way, n, u)
                    total = total + ring[h, way, n, half_rows(u), :]
            return total

        sent(0, h, part.at[pl.ds(0, NZ)])
        if h + 1 < HOPS:
            def spread(u, source, device, arrival):
                block = block_at(h, u, source)
                remote(block, block, sent_sem.at[1, h], arrival, (device, q)).start()

            for u in range(2):
                state[h, p, half_rows(u), :] = finished(u)
                for d in (1, 3, 2):
                    spread(u, p, across(u, d), first_sem.at[h, u, NX - d - 1])
                for e in (1, 3, 2):
                    spread(u, p, across(1 - u, e), group_sem.at[h, 0])
            for d in (1, 3, 2):
                for u in range(2):
                    arrived(h, u, d)
                    for e in (1, 3, 2):
                        spread(u, across(u, d), across(1 - u, e), group_sem.at[h, d])
        else:
            for u in range(2):
                out[half_rows(u), :] = finished(u)

    owned = out[...]
    top_row = pl.ds(0, 1)
    col_tot[q, top_row, :] = jnp.sum(owned * owned, axis=0, keepdims=True)

    far_first = (8, 7, 9, 6, 10, 5, 11, 4, 12, 3, 13, 2, 14, 1, 15)
    for stage, (tot, me) in enumerate(((col_tot, q), (row_tot, p))):
        for d in far_first:
            device = (p, (q + d) % NCOL) if stage == 0 else ((p + d) % NROW, q)
            remote(tot.at[me, top_row], tot.at[me, top_row], tot_sem.at[0, stage], tot_sem.at[1, stage], device).start()
        every = tot.at[pl.ds(0, 15), top_row]
        remote(every, every, tot_sem.at[0, stage], tot_sem.at[1, stage], (p, z * 2 + other)).wait()
        if stage == 0:
            row_tot[p, top_row, :] = jnp.sum(col_tot[:, top_row, :], axis=0)
    totals = jnp.sum(row_tot[:, top_row, :], axis=0)
    out[...] = owned * lax.rsqrt(totals / ENTITIES + 1e-06)
    for h in range(HOPS):
        sent(2, h, cross.at[0, pl.ds(0, 7)])
    for h in range(HOPS - 1):
        sent(1, h, state.at[0, pl.ds(0, NROW - 1)])


def run_chain(table, first, cells):
    vmem = pl.BlockSpec(memory_space=pltpu.VMEM)
    hbm = pl.BlockSpec(memory_space=pltpu.HBM)
    return pl.pallas_call(
        chain_kernel,
        out_shape=jax.ShapeDtypeStruct((BLOCK, QUERIES), F32),
        in_specs=[hbm] * 3,
        out_specs=vmem,
        scratch_shapes=[
            pltpu.SMEM((HOPS * 8, 128), jnp.int32),
            pltpu.VMEM((SLOTS + 1, TILE, 2 * TILE), F32),
            pltpu.VMEM((SLOTS + 1, TILE, 2 * TILE), F32),
            pltpu.VMEM((NROW, NCOL * BLOCK, BLOCK), BF16),
            pltpu.VMEM((NROW, NCOL * BLOCK, BLOCK), BF16),
            pltpu.VMEM((NY * BLOCK, 2 * QUERIES), BF16),
            pltpu.VMEM((NCOL, BLOCK, QUERIES), F32),
            pltpu.VMEM((HOPS, NZ, BLOCK, QUERIES), F32),
            pltpu.VMEM((HOPS, 2, 4, BLOCK, QUERIES), F32),
            pltpu.VMEM((HOPS - 1, NROW, BLOCK, QUERIES), F32),
            pltpu.VMEM((NCOL, 8, QUERIES), F32),
            pltpu.VMEM((NROW, 8, QUERIES), F32),
            pltpu.SemaphoreType.DMA((4,)),
            pltpu.SemaphoreType.DMA((3, HOPS)),
            pltpu.SemaphoreType.DMA((HOPS, NZ)),
            pltpu.SemaphoreType.DMA((HOPS, 2, 4, 2)),
            pltpu.SemaphoreType.DMA((HOPS - 1, 2, NX - 1)),
            pltpu.SemaphoreType.DMA((HOPS - 1, NX)),
            pltpu.SemaphoreType.DMA((2, 2)),
        ],
        compiler_params=pltpu.CompilerParams(
            collective_id=0, has_side_effects=True, vmem_limit_bytes=60 * 2**20
        ),
        name="relation_chain",
    )(table, first, cells)


def shards(tiles, tile_coords, tile_count, seeds, chain):
    cells, table, product = merge(
        chain, tile_count[0, 0], tile_coords[0, 0], seeds.reshape(1, QUERIES), tiles[0, 0]
    )
    return run_chain(table, product.reshape(NCOL, BLOCK, QUERIES), cells)


def solution(mesh):
    in_specs = (
        P("row", "col", None, None, None, None),
        P("row", "col", None, None, None),
        P("row", "col", None),
        P(),
        P(),
    )
    out_specs = P(("row", "col"), None)
    return jax.shard_map(shards, mesh=mesh, in_specs=in_specs, out_specs=out_specs, check_vma=False)
```

```python
import jax
import jax.numpy as jnp
from jax import lax
from jax.experimental import pallas as pl
from jax.experimental.pallas import tpu as pltpu
from jax.sharding import PartitionSpec as P

QUERIES = 128
TILE = 64
BLOCK = 128
SLOTS = 256
HOPS = 3
NX, NY, NZ = 4, 4, 8
NROW = NX * NY
NCOL = NZ * 2
CELLS = 2 * NCOL * NROW
ENTITIES = NROW * NCOL * BLOCK
MESH = pl.DeviceIdType.MESH
F32 = jnp.float32
BF16 = jnp.bfloat16


def merge_kernel(
    chain_hbm, count_hbm, coords_hbm, seeds_hbm, tiles, cells, plan_hbm, product_hbm,
    chain, count, coords, seeds, plan, product, slots, merged, rows, seed_rows, small_sem, in_sem, out_sem, plan_sem,
):
    pairs = ((chain_hbm, chain), (count_hbm, count), (coords_hbm, coords), (seeds_hbm, seeds))
    small = [pltpu.make_async_copy(src, dst, small_sem.at[n]) for n, (src, dst) in enumerate(pairs)]
    for copy in small:
        copy.start()
    product[...] = jnp.zeros_like(product)
    small[0].wait()
    order = (1, 2, 0)
    loads = {}
    for h in order:
        loads[h] = pltpu.make_async_copy(tiles.at[chain[h]], slots.at[h], in_sem.at[h])
        loads[h].start()
    for copy in small[1:]:
        copy.wait()
    lane = lax.broadcasted_iota(jnp.int32, (SLOTS, SLOTS), 1)
    line = lax.broadcasted_iota(jnp.int32, (SLOTS, SLOTS), 0)
    slot = lax.broadcasted_iota(jnp.int32, (1, SLOTS), 1)
    for h in range(HOPS):
        pair = coords[chain[h]]
        i, j = pair[0:1, :], pair[1:2, :]
        block = ((i >> 1) & 1) * 16 + (i >> 2) * 2 + (i & 1)
        if h == 0:
            word = block + (j << 8)
        else:
            along_x, along_y = j >> 3, (j >> 1) & 3
            second = (j & 1) == 1
            couple = jnp.where(second, 8 + along_y * 2 + (along_x >> 1), along_x * 2 + (along_y >> 1))
            side = jnp.where(second, along_x & 1, along_y & 1)
            key = jnp.where(slot < count[chain[h]], block * NROW + couple, CELLS + slot)
            keys = jnp.sum(jnp.where(lane == line, key, 0), axis=1, keepdims=True)
            first = jnp.min(jnp.where(keys == key, line, SLOTS), axis=0, keepdims=True)
            word = first + (jnp.where(first == slot, SLOTS, first) << 9) + (side << 18)
            for n in range(CELLS // 128):
                cell = lane[:, :128] + n * 128
                found = jnp.where(keys == cell, line[:, :128], SLOTS)
                rows[h * 8 + n:h * 8 + n + 1, :] = jnp.min(found, axis=0, keepdims=True)
        for n in range(SLOTS // 128):
            rows[h * 8 + 4 + n:h * 8 + 5 + n, :] = word[:, n * 128:(n + 1) * 128]
    copy = pltpu.make_async_copy(rows, plan, plan_sem.at[0])
    copy.start()
    stores = [pltpu.make_async_copy(rows, plan_hbm, plan_sem.at[1])]
    stores[0].start()
    q = lax.axis_index("col")
    offsets = lax.broadcasted_iota(jnp.int32, (TILE, QUERIES), 0)
    for j in range(2 * NROW):
        ids = ((j // 2) * NCOL + q) * BLOCK + (j % 2) * TILE + offsets
        seed_rows[j] = jnp.where(ids == seeds[...], 1.0, 0.0).astype(BF16)
    copy.wait()
    side_of = lax.broadcasted_iota(jnp.int32, (TILE, 2 * TILE), 1) >> 6
    for h in (1, 2):
        merged[h - 1, SLOTS] = jnp.zeros((TILE, 2 * TILE), F32)
        loads[h].wait()

        @pl.loop(0, count[chain[h]] // 32)
        def _(n):
            for u in range(16):
                value = slots[h, n * 16 + u]
                swapped = pltpu.roll(value, TILE, 1)
                for k in range(2):
                    t = n * 32 + u * 2 + k
                    word = plan[h * 8 + 4 + (t >> 7), t & 127]
                    side = word >> 18
                    base = merged[h - 1, (word >> 9) & 511]
                    moved = jnp.where(side == k, value, swapped)
                    merged[h - 1, word & 511] = base + jnp.where(side_of == side, moved, 0.0)

        copy = pltpu.make_async_copy(merged.at[h - 1], cells.at[h - 1], out_sem.at[h - 1])
        copy.start()
        stores.append(copy)
    loads[0].wait()
    none = jnp.zeros((TILE, QUERIES), BF16)

    @pl.loop(0, count[chain[0]] // 32)
    def _(n):
        for u in range(16):
            value = slots[0, n * 16 + u]
            top = value.astype(BF16)
            low = (value - top.astype(F32)).astype(BF16)
            t = n * 32 + u * 2
            words = [plan[4 + ((t + k) >> 7), (t + k) & 127] for k in range(2)]
            left = jnp.concatenate([seed_rows[words[0] >> 8], none], axis=0)
            right = jnp.concatenate([none, seed_rows[words[1] >> 8]], axis=0)
            both = jnp.dot(
                jnp.concatenate([top, low], axis=0), jnp.concatenate([left, right], axis=1), preferred_element_type=F32
            )
            both = both[:TILE] + both[TILE:]
            for k in range(2):
                at = words[k] & 255
                product[at] = product[at] + both[:, k * QUERIES:(k + 1) * QUERIES]

    copy = pltpu.make_async_copy(product, product_hbm, plan_sem.at[2])
    copy.start()
    stores.append(copy)
    for copy in stores:
        copy.wait()


def merge(chain, count, coords, seeds, tiles):
    hbm = pl.BlockSpec(memory_space=pltpu.HBM)
    return pl.pallas_call(
        merge_kernel,
        out_shape=(
            jax.ShapeDtypeStruct((HOPS - 1, SLOTS + 1, TILE, 2 * TILE), F32),
            jax.ShapeDtypeStruct((HOPS * 8, 128), jnp.int32),
            jax.ShapeDtypeStruct((2 * NCOL, TILE, QUERIES), F32),
        ),
        in_specs=[hbm] * 5,
        out_specs=(hbm, hbm, hbm),
        scratch_shapes=[
            pltpu.SMEM((HOPS,), jnp.int32),
            pltpu.SMEM((HOPS,), jnp.int32),
            pltpu.VMEM((HOPS, 2, SLOTS), jnp.int32),
            pltpu.VMEM((1, QUERIES), jnp.int32),
            pltpu.SMEM((HOPS * 8, 128), jnp.int32),
            pltpu.VMEM((2 * NCOL, TILE, QUERIES), F32),
            pltpu.VMEM((HOPS, SLOTS // 2, TILE, 2 * TILE), F32),
            pltpu.VMEM((HOPS - 1, SLOTS + 1, TILE, 2 * TILE), F32),
            pltpu.VMEM((HOPS * 8, 128), jnp.int32),
            pltpu.VMEM((2 * NROW, TILE, QUERIES), BF16),
            pltpu.SemaphoreType.DMA((4,)),
            pltpu.SemaphoreType.DMA((HOPS,)),
            pltpu.SemaphoreType.DMA((HOPS - 1,)),
            pltpu.SemaphoreType.DMA((3,)),
        ],
        compiler_params=pltpu.CompilerParams(vmem_limit_bytes=60 * 2**20),
        name="first_hop_and_cells",
    )(chain, count, coords, seeds, tiles)


def chain_kernel(
    table_hbm, first, cells, out,
    table, held_a, held_b, dense_hi, dense_lo, right, part, cross, ring, state, col_tot, row_tot,
    load_sem, sent_sem, cross_sem, ring_sem, first_sem, group_sem, tot_sem,
):
    p = lax.axis_index("row")
    q = lax.axis_index("col")
    x, y = p // NY, p % NY
    z, core = q // 2, q % 2
    other = 1 - core
    held = (None, held_a, held_b)

    def remote(src, dst, send, recv, device):
        return pltpu.make_async_remote_copy(
            src_ref=src, dst_ref=dst, send_sem=send, recv_sem=recv, device_id=device, device_id_type=MESH
        )

    def load(h):
        return pltpu.make_async_copy(cells.at[h - 1], held[h], load_sem.at[h - 1])

    barrier = pltpu.get_barrier_semaphore()

    @pl.loop(1, 16)
    def _(d):
        pl.semaphore_signal(barrier, inc=1, device_id=(p, (q + d) % NCOL), device_id_type=MESH)
        pl.semaphore_signal(barrier, inc=1, device_id=((p + d) % NROW, q), device_id_type=MESH)

    fetches = [
        pltpu.make_async_copy(first, part, load_sem.at[2]), pltpu.make_async_copy(table_hbm, table, load_sem.at[3]),
    ]
    for copy in fetches:
        copy.start()
    load(1).start()
    load(2).start()

    def assemble(h, start, stop):
        @pl.loop(start, stop)
        def _(block):
            rows = pl.ds(pl.multiple_of(block * TILE, TILE), TILE)
            for s in range(NROW):
                value = held[h][table[h * 8 + (block >> 3), (block & 7) * NROW + s]]
                top = value.astype(BF16)
                dense_hi[s, rows, :] = top
                dense_lo[s, rows, :] = (value - top.astype(F32)).astype(BF16)

    def split(h, d):
        gx, gy = (x + d) % NX, (y + d) % NY
        for u in range(2):
            for k in range(NX):
                value = state[h - 1, gx * NY + k if u == 0 else k * NY + gy, u * TILE:(u + 1) * TILE, :]
                top = value.astype(BF16)
                at = (u * NX + k) * TILE
                right[at:at + TILE, :QUERIES] = top
                right[at:at + TILE, QUERIES:] = (value - top.astype(F32)).astype(BF16)

    def multiply(d, start, steps, size=8):
        gx, gy = (x + d) % NX, (y + d) % NY
        couples = (gx * 2, gx * 2 + 1, 8 + gy * 2, 9 + gy * 2)

        @pl.loop(0, steps)
        def _(m):
            at = start + m * size
            rows = pl.ds(pl.multiple_of(at * BLOCK, size * BLOCK), size * BLOCK)
            left = jnp.concatenate([dense_hi[c, rows, :] for c in couples], axis=1)
            both = jnp.dot(left, right[...], preferred_element_type=F32)
            left = jnp.concatenate([dense_lo[c, rows, :] for c in couples], axis=1)
            low = jnp.dot(left, right[:, :QUERIES], preferred_element_type=F32)
            total = both[:, :QUERIES] + both[:, QUERIES:] + low
            part[pl.ds(at, size)] = part[pl.ds(at, size)] + total.reshape(size, BLOCK, QUERIES)

    def half_rows(u):
        return pl.ds(u * TILE, TILE)

    def away(way, k):
        return (z + (k if way == 0 else NZ - k)) % NZ

    for copy in fetches:
        copy.wait()
    pl.semaphore_wait(barrier, 30)

    def sent(kind, h, ref):
        remote(ref, ref, sent_sem.at[kind, h], sent_sem.at[kind, h], (p, z * 2 + other)).wait_send()

    def block_at(h, u, source):
        return state.at[h, source, half_rows(u)]

    def across(u, d):
        return ((x + d) % NX) * NY + y if u == 0 else x * NY + (y + d) % NY

    def arrived(h, u, d):
        source = block_at(h, u, across(u, d))
        remote(source, source, sent_sem.at[1, h], first_sem.at[h, u, d - 1], (p, z * 2 + other)).wait_recv()

    def group_arrived(h, d):
        six = state.at[h, pl.ds(0, 3)]
        remote(six, six, sent_sem.at[1, h], group_sem.at[h, d], (p, z * 2 + other)).wait_recv()

    for h in range(HOPS):

        def crossing(block):
            return remote(
                part.at[other * 8 + block], cross.at[h, block],
                sent_sem.at[0, h], cross_sem.at[h, block], (p, z * 2 + other),
            )

        order = (4, 3, 5, 1, 7, 2, 6, 0)
        if h > 0:
            def columns(d):
                group_arrived(h - 1, d)
                split(h, d)

            part[...] = jnp.zeros_like(part)

            @pl.loop(0, NX - 1)
            def _(n):
                columns(n + n // 2)
                multiply(n + n // 2, 0, 2)

            columns(2)
            for n in (1, 0):
                four = (z // 4 + n) % 2 * 4
                multiply(2, other * 8 + four, 1, 4)
                for k in range(4):
                    crossing(four + (z + k) % 4).start()
            multiply(2, core * 8, 1)
        else:
            for o in order:
                crossing((z + o) % NZ).start()

        def sum_of(o):
            return cross.at[h, (z + o) % NZ]

        def along(way, n, u, src, k):
            return remote(
                src, ring.at[h, way, n, half_rows(u)],
                sent_sem.at[2, h], ring_sem.at[h, way, n, u], (p, away(way, k) * 2 + core),
            )

        def got(way, n, u):
            along(way, n, u, ring.at[h, way, n, half_rows(u)], 1).wait_recv()

        for o in order:
            block = (z + o) % NZ
            crossing(block).wait_recv()
            cross[h, block] = cross[h, block] + part[core * 8 + block]
            if o == 4:
                along(0, 3, 0, sum_of(4).at[half_rows(0)], 2).start()
                along(1, 3, 1, sum_of(4).at[half_rows(1)], 2).start()
            elif o in (3, 5):
                for u in range(2):
                    along(o // 4, 2, u, sum_of(o).at[half_rows(u)], 1).start()
            elif o in (1, 7):
                for u in range(2):
                    along(o // 4, 0, u, sum_of(o).at[half_rows(u)], 1).start()
        if h + 1 < HOPS:
            load(h + 1).wait()
            assemble(h + 1, 0, 16)
        for u in range(2):
            for way in range(2):
                got(way, 2, u)
                total = ring[h, way, 2, half_rows(u), :] + cross[h, away(way, 2), half_rows(u), :]
                if u == way:
                    got(way, 3, u)
                    total = total + ring[h, way, 3, half_rows(u), :]
                ring[h, way, 2, half_rows(u), :] = total
                along(way, 1, u, ring.at[h, way, 2, half_rows(u)], 2).start()
        if h + 1 < HOPS:
            assemble(h + 1, 16, 32)

        def finished(u):
            total = cross[h, z, half_rows(u), :]
            for n in (0, 1):
                for way in range(2):
                    got(way, n, u)
                    total = total + ring[h, way, n, half_rows(u), :]
            return total

        sent(0, h, part.at[pl.ds(0, NZ)])
        if h + 1 < HOPS:
            def spread(u, source, device, arrival):
                block = block_at(h, u, source)
                remote(block, block, sent_sem.at[1, h], arrival, (device, q)).start()

            for u in range(2):
                state[h, p, half_rows(u), :] = finished(u)
                for d in (1, 3, 2):
                    spread(u, p, across(u, d), first_sem.at[h, u, NX - d - 1])
                for e in (1, 3, 2):
                    spread(u, p, across(1 - u, e), group_sem.at[h, 0])
            for d in (1, 3, 2):
                for u in range(2):
                    arrived(h, u, d)
                    for e in (1, 3, 2):
                        spread(u, across(u, d), across(1 - u, e), group_sem.at[h, d])
        else:
            for u in range(2):
                out[half_rows(u), :] = finished(u)

    owned = out[...]
    top_row = pl.ds(0, 1)
    col_tot[q, top_row, :] = jnp.sum(owned * owned, axis=0, keepdims=True)

    far_first = (8, 7, 9, 6, 10, 5, 11, 4, 12, 3, 13, 2, 14, 1, 15)
    for stage, (tot, me) in enumerate(((col_tot, q), (row_tot, p))):
        for d in far_first:
            device = (p, (q + d) % NCOL) if stage == 0 else ((p + d) % NROW, q)
            remote(tot.at[me, top_row], tot.at[me, top_row], tot_sem.at[0, stage], tot_sem.at[1, stage], device).start()
        every = tot.at[pl.ds(0, 15), top_row]
        remote(every, every, tot_sem.at[0, stage], tot_sem.at[1, stage], (p, z * 2 + other)).wait()
        if stage == 0:
            row_tot[p, top_row, :] = jnp.sum(col_tot[:, top_row, :], axis=0)
    totals = jnp.sum(row_tot[:, top_row, :], axis=0)
    out[...] = owned * lax.rsqrt(totals / ENTITIES + 1e-06)
    for h in range(HOPS):
        sent(2, h, cross.at[0, pl.ds(0, 7)])
    for h in range(HOPS - 1):
        sent(1, h, state.at[0, pl.ds(0, NROW - 1)])


def run_chain(table, first, cells):
    vmem = pl.BlockSpec(memory_space=pltpu.VMEM)
    hbm = pl.BlockSpec(memory_space=pltpu.HBM)
    return pl.pallas_call(
        chain_kernel,
        out_shape=jax.ShapeDtypeStruct((BLOCK, QUERIES), F32),
        in_specs=[hbm] * 3,
        out_specs=vmem,
        scratch_shapes=[
            pltpu.SMEM((HOPS * 8, 128), jnp.int32),
            pltpu.VMEM((SLOTS + 1, TILE, 2 * TILE), F32),
            pltpu.VMEM((SLOTS + 1, TILE, 2 * TILE), F32),
            pltpu.VMEM((NROW, NCOL * BLOCK, BLOCK), BF16),
            pltpu.VMEM((NROW, NCOL * BLOCK, BLOCK), BF16),
            pltpu.VMEM((NY * BLOCK, 2 * QUERIES), BF16),
            pltpu.VMEM((NCOL, BLOCK, QUERIES), F32),
            pltpu.VMEM((HOPS, NZ, BLOCK, QUERIES), F32),
            pltpu.VMEM((HOPS, 2, 4, BLOCK, QUERIES), F32),
            pltpu.VMEM((HOPS - 1, NROW, BLOCK, QUERIES), F32),
            pltpu.VMEM((NCOL, 8, QUERIES), F32),
            pltpu.VMEM((NROW, 8, QUERIES), F32),
            pltpu.SemaphoreType.DMA((4,)),
            pltpu.SemaphoreType.DMA((3, HOPS)),
            pltpu.SemaphoreType.DMA((HOPS, NZ)),
            pltpu.SemaphoreType.DMA((HOPS, 2, 4, 2)),
            pltpu.SemaphoreType.DMA((HOPS - 1, 2, NX - 1)),
            pltpu.SemaphoreType.DMA((HOPS - 1, NX)),
            pltpu.SemaphoreType.DMA((2, 2)),
        ],
        compiler_params=pltpu.CompilerParams(
            collective_id=0, has_side_effects=True, vmem_limit_bytes=60 * 2**20
        ),
        name="relation_chain",
    )(table, first, cells)


def shards(tiles, tile_coords, tile_count, seeds, chain):
    cells, table, product = merge(
        chain, tile_count[0, 0], tile_coords[0, 0], seeds.reshape(1, QUERIES), tiles[0, 0]
    )
    return run_chain(table, product.reshape(NCOL, BLOCK, QUERIES), cells)


def solution(mesh):
    in_specs = (
        P("row", "col", None, None, None, None),
        P("row", "col", None, None, None),
        P("row", "col", None),
        P(),
        P(),
    )
    out_specs = P(("row", "col"), None)
    return jax.shard_map(shards, mesh=mesh, in_specs=in_specs, out_specs=out_specs, check_vma=False)
```

```python
import jax
import jax.numpy as jnp
from jax import lax
from jax.experimental import pallas as pl
from jax.experimental.pallas import tpu as pltpu
from jax.sharding import PartitionSpec as P

QUERIES = 128
TILE = 64
BLOCK = 128
SLOTS = 256
HOPS = 3
NX, NY, NZ = 4, 4, 8
NROW = NX * NY
NCOL = NZ * 2
CELLS = 2 * NCOL * NROW
ENTITIES = NROW * NCOL * BLOCK
MESH = pl.DeviceIdType.MESH
F32 = jnp.float32
BF16 = jnp.bfloat16


def merge_kernel(
    chain_hbm, count_hbm, coords_hbm, seeds_hbm, tiles, cells, plan_hbm, product_hbm,
    chain, count, coords, seeds, plan, product, slots, merged, rows, seed_rows, small_sem, in_sem, out_sem, plan_sem,
):
    pairs = ((chain_hbm, chain), (count_hbm, count), (coords_hbm, coords), (seeds_hbm, seeds))
    small = [pltpu.make_async_copy(src, dst, small_sem.at[n]) for n, (src, dst) in enumerate(pairs)]
    for copy in small:
        copy.start()
    product[...] = jnp.zeros_like(product)
    small[0].wait()
    order = (1, 2, 0)
    loads = {}
    for h in order:
        loads[h] = pltpu.make_async_copy(tiles.at[chain[h]], slots.at[h], in_sem.at[h])
        loads[h].start()
    for copy in small[1:]:
        copy.wait()
    lane = lax.broadcasted_iota(jnp.int32, (SLOTS, SLOTS), 1)
    line = lax.broadcasted_iota(jnp.int32, (SLOTS, SLOTS), 0)
    slot = lax.broadcasted_iota(jnp.int32, (1, SLOTS), 1)
    for h in range(HOPS):
        pair = coords[chain[h]]
        i, j = pair[0:1, :], pair[1:2, :]
        block = ((i >> 1) & 1) * 16 + (i >> 2) * 2 + (i & 1)
        if h == 0:
            word = block + (j << 8)
        else:
            along_x, along_y = j >> 3, (j >> 1) & 3
            second = (j & 1) == 1
            couple = jnp.where(second, 8 + along_y * 2 + (along_x >> 1), along_x * 2 + (along_y >> 1))
            side = jnp.where(second, along_x & 1, along_y & 1)
            key = jnp.where(slot < count[chain[h]], block * NROW + couple, CELLS + slot)
            keys = jnp.sum(jnp.where(lane == line, key, 0), axis=1, keepdims=True)
            first = jnp.min(jnp.where(keys == key, line, SLOTS), axis=0, keepdims=True)
            word = first + (jnp.where(first == slot, SLOTS, first) << 9) + (side << 18)
            for n in range(CELLS // 128):
                cell = lane[:, :128] + n * 128
                found = jnp.where(keys == cell, line[:, :128], SLOTS)
                rows[h * 8 + n:h * 8 + n + 1, :] = jnp.min(found, axis=0, keepdims=True)
        for n in range(SLOTS // 128):
            rows[h * 8 + 4 + n:h * 8 + 5 + n, :] = word[:, n * 128:(n + 1) * 128]
    copy = pltpu.make_async_copy(rows, plan, plan_sem.at[0])
    copy.start()
    stores = [pltpu.make_async_copy(rows, plan_hbm, plan_sem.at[1])]
    stores[0].start()
    q = lax.axis_index("col")
    offsets = lax.broadcasted_iota(jnp.int32, (TILE, QUERIES), 0)
    for j in range(2 * NROW):
        ids = ((j // 2) * NCOL + q) * BLOCK + (j % 2) * TILE + offsets
        seed_rows[j] = jnp.where(ids == seeds[...], 1.0, 0.0).astype(BF16)
    copy.wait()
    side_of = lax.broadcasted_iota(jnp.int32, (TILE, 2 * TILE), 1) >> 6
    for h in (1, 2):
        merged[h - 1, SLOTS] = jnp.zeros((TILE, 2 * TILE), F32)
        loads[h].wait()

        @pl.loop(0, count[chain[h]] // 32)
        def _(n):
            for u in range(16):
                value = slots[h, n * 16 + u]
                swapped = pltpu.roll(value, TILE, 1)
                for k in range(2):
                    t = n * 32 + u * 2 + k
                    word = plan[h * 8 + 4 + (t >> 7), t & 127]
                    side = word >> 18
                    base = merged[h - 1, (word >> 9) & 511]
                    moved = jnp.where(side == k, value, swapped)
                    merged[h - 1, word & 511] = base + jnp.where(side_of == side, moved, 0.0)

        copy = pltpu.make_async_copy(merged.at[h - 1], cells.at[h - 1], out_sem.at[h - 1])
        copy.start()
        stores.append(copy)
    loads[0].wait()
    none = jnp.zeros((TILE, QUERIES), BF16)

    @pl.loop(0, count[chain[0]] // 32)
    def _(n):
        for u in range(16):
            value = slots[0, n * 16 + u]
            top = value.astype(BF16)
            low = (value - top.astype(F32)).astype(BF16)
            t = n * 32 + u * 2
            words = [plan[4 + ((t + k) >> 7), (t + k) & 127] for k in range(2)]
            left = jnp.concatenate([seed_rows[words[0] >> 8], none], axis=0)
            right = jnp.concatenate([none, seed_rows[words[1] >> 8]], axis=0)
            both = jnp.dot(
                jnp.concatenate([top, low], axis=0), jnp.concatenate([left, right], axis=1), preferred_element_type=F32
            )
            both = both[:TILE] + both[TILE:]
            for k in range(2):
                at = words[k] & 255
                product[at] = product[at] + both[:, k * QUERIES:(k + 1) * QUERIES]

    copy = pltpu.make_async_copy(product, product_hbm, plan_sem.at[2])
    copy.start()
    stores.append(copy)
    for copy in stores:
        copy.wait()


def merge(chain, count, coords, seeds, tiles):
    hbm = pl.BlockSpec(memory_space=pltpu.HBM)
    return pl.pallas_call(
        merge_kernel,
        out_shape=(
            jax.ShapeDtypeStruct((HOPS - 1, SLOTS + 1, TILE, 2 * TILE), F32),
            jax.ShapeDtypeStruct((HOPS * 8, 128), jnp.int32),
            jax.ShapeDtypeStruct((2 * NCOL, TILE, QUERIES), F32),
        ),
        in_specs=[hbm] * 5,
        out_specs=(hbm, hbm, hbm),
        scratch_shapes=[
            pltpu.SMEM((HOPS,), jnp.int32),
            pltpu.SMEM((HOPS,), jnp.int32),
            pltpu.VMEM((HOPS, 2, SLOTS), jnp.int32),
            pltpu.VMEM((1, QUERIES), jnp.int32),
            pltpu.SMEM((HOPS * 8, 128), jnp.int32),
            pltpu.VMEM((2 * NCOL, TILE, QUERIES), F32),
            pltpu.VMEM((HOPS, SLOTS // 2, TILE, 2 * TILE), F32),
            pltpu.VMEM((HOPS - 1, SLOTS + 1, TILE, 2 * TILE), F32),
            pltpu.VMEM((HOPS * 8, 128), jnp.int32),
            pltpu.VMEM((2 * NROW, TILE, QUERIES), BF16),
            pltpu.SemaphoreType.DMA((4,)),
            pltpu.SemaphoreType.DMA((HOPS,)),
            pltpu.SemaphoreType.DMA((HOPS - 1,)),
            pltpu.SemaphoreType.DMA((3,)),
        ],
        compiler_params=pltpu.CompilerParams(vmem_limit_bytes=60 * 2**20),
        name="first_hop_and_cells",
    )(chain, count, coords, seeds, tiles)


def chain_kernel(
    table_hbm, first, cells, out,
    table, held_a, held_b, dense_hi, dense_lo, right, part, cross, ring, state, col_tot, row_tot,
    load_sem, sent_sem, cross_sem, ring_sem, first_sem, group_sem, tot_sem,
):
    p = lax.axis_index("row")
    q = lax.axis_index("col")
    x, y = p // NY, p % NY
    z, core = q // 2, q % 2
    other = 1 - core
    held = (None, held_a, held_b)

    def remote(src, dst, send, recv, device):
        return pltpu.make_async_remote_copy(
            src_ref=src, dst_ref=dst, send_sem=send, recv_sem=recv, device_id=device, device_id_type=MESH
        )

    def load(h):
        return pltpu.make_async_copy(cells.at[h - 1], held[h], load_sem.at[h - 1])

    barrier = pltpu.get_barrier_semaphore()

    @pl.loop(1, 16)
    def _(d):
        pl.semaphore_signal(barrier, inc=1, device_id=(p, (q + d) % NCOL), device_id_type=MESH)
        pl.semaphore_signal(barrier, inc=1, device_id=((p + d) % NROW, q), device_id_type=MESH)

    fetches = [
        pltpu.make_async_copy(first, part, load_sem.at[2]), pltpu.make_async_copy(table_hbm, table, load_sem.at[3]),
    ]
    for copy in fetches:
        copy.start()
    load(1).start()
    load(2).start()

    def assemble(h, start, stop):
        @pl.loop(start, stop)
        def _(block):
            rows = pl.ds(pl.multiple_of(block * TILE, TILE), TILE)
            for s in range(NROW):
                value = held[h][table[h * 8 + (block >> 3), (block & 7) * NROW + s]]
                top = value.astype(BF16)
                dense_hi[s, rows, :] = top
                dense_lo[s, rows, :] = (value - top.astype(F32)).astype(BF16)

    def split(h, d):
        gx, gy = (x + d) % NX, (y + d) % NY
        for u in range(2):
            for k in range(NX):
                value = state[h - 1, gx * NY + k if u == 0 else k * NY + gy, u * TILE:(u + 1) * TILE, :]
                top = value.astype(BF16)
                at = (u * NX + k) * TILE
                right[at:at + TILE, :QUERIES] = top
                right[at:at + TILE, QUERIES:] = (value - top.astype(F32)).astype(BF16)

    def multiply(d, start, steps, size=8):
        gx, gy = (x + d) % NX, (y + d) % NY
        couples = (gx * 2, gx * 2 + 1, 8 + gy * 2, 9 + gy * 2)

        @pl.loop(0, steps)
        def _(m):
            at = start + m * size
            rows = pl.ds(pl.multiple_of(at * BLOCK, size * BLOCK), size * BLOCK)
            left = jnp.concatenate([dense_hi[c, rows, :] for c in couples], axis=1)
            both = jnp.dot(left, right[...], preferred_element_type=F32)
            left = jnp.concatenate([dense_lo[c, rows, :] for c in couples], axis=1)
            low = jnp.dot(left, right[:, :QUERIES], preferred_element_type=F32)
            total = both[:, :QUERIES] + both[:, QUERIES:] + low
            part[pl.ds(at, size)] = part[pl.ds(at, size)] + total.reshape(size, BLOCK, QUERIES)

    def half_rows(u):
        return pl.ds(u * TILE, TILE)

    def away(way, k):
        return (z + (k if way == 0 else NZ - k)) % NZ

    for copy in fetches:
        copy.wait()
    pl.semaphore_wait(barrier, 30)

    def sent(kind, h, ref):
        remote(ref, ref, sent_sem.at[kind, h], sent_sem.at[kind, h], (p, z * 2 + other)).wait_send()

    def block_at(h, u, source):
        return state.at[h, source, half_rows(u)]

    def across(u, d):
        return ((x + d) % NX) * NY + y if u == 0 else x * NY + (y + d) % NY

    def arrived(h, u, d):
        source = block_at(h, u, across(u, d))
        remote(source, source, sent_sem.at[1, h], first_sem.at[h, u, d - 1], (p, z * 2 + other)).wait_recv()

    def group_arrived(h, d):
        six = state.at[h, pl.ds(0, 3)]
        remote(six, six, sent_sem.at[1, h], group_sem.at[h, d], (p, z * 2 + other)).wait_recv()

    for h in range(HOPS):

        def crossing(block):
            return remote(
                part.at[other * 8 + block], cross.at[h, block],
                sent_sem.at[0, h], cross_sem.at[h, block], (p, z * 2 + other),
            )

        order = (4, 3, 5, 1, 7, 2, 6, 0)
        if h > 0:
            def columns(d):
                group_arrived(h - 1, d)
                split(h, d)

            part[...] = jnp.zeros_like(part)

            @pl.loop(0, NX - 1)
            def _(n):
                columns(n + n // 2)
                multiply(n + n // 2, 0, 2)

            columns(2)
            for n in (1, 0):
                four = (z // 4 + n) % 2 * 4
                multiply(2, other * 8 + four, 1, 4)
                for k in range(4):
                    crossing(four + (z + k) % 4).start()
            multiply(2, core * 8, 1)
        else:
            for o in order:
                crossing((z + o) % NZ).start()

        def sum_of(o):
            return cross.at[h, (z + o) % NZ]

        def along(way, n, u, src, k):
            return remote(
                src, ring.at[h, way, n, half_rows(u)],
                sent_sem.at[2, h], ring_sem.at[h, way, n, u], (p, away(way, k) * 2 + core),
            )

        def got(way, n, u):
            along(way, n, u, ring.at[h, way, n, half_rows(u)], 1).wait_recv()

        for o in order:
            block = (z + o) % NZ
            crossing(block).wait_recv()
            cross[h, block] = cross[h, block] + part[core * 8 + block]
            if o == 4:
                along(0, 3, 0, sum_of(4).at[half_rows(0)], 2).start()
                along(1, 3, 1, sum_of(4).at[half_rows(1)], 2).start()
            elif o in (3, 5):
                for u in range(2):
                    along(o // 4, 2, u, sum_of(o).at[half_rows(u)], 1).start()
            elif o in (1, 7):
                for u in range(2):
                    along(o // 4, 0, u, sum_of(o).at[half_rows(u)], 1).start()
        if h + 1 < HOPS:
            load(h + 1).wait()
            assemble(h + 1, 0, 16)
        for u in range(2):
            for way in range(2):
                got(way, 2, u)
                total = ring[h, way, 2, half_rows(u), :] + cross[h, away(way, 2), half_rows(u), :]
                if u == way:
                    got(way, 3, u)
                    total = total + ring[h, way, 3, half_rows(u), :]
                ring[h, way, 2, half_rows(u), :] = total
                along(way, 1, u, ring.at[h, way, 2, half_rows(u)], 2).start()
        if h + 1 < HOPS:
            assemble(h + 1, 16, 32)

        def finished(u):
            total = cross[h, z, half_rows(u), :]
            for n in (0, 1):
                for way in range(2):
                    got(way, n, u)
                    total = total + ring[h, way, n, half_rows(u), :]
            return total

        sent(0, h, part.at[pl.ds(0, NZ)])
        if h + 1 < HOPS:
            def spread(u, source, device, arrival):
                block = block_at(h, u, source)
                remote(block, block, sent_sem.at[1, h], arrival, (device, q)).start()

            for u in range(2):
                state[h, p, half_rows(u), :] = finished(u)
                for d in (1, 3, 2):
                    spread(u, p, across(u, d), first_sem.at[h, u, NX - d - 1])
                for e in (1, 3, 2):
                    spread(u, p, across(1 - u, e), group_sem.at[h, 0])
            for u, d in ((0, 1), (0, 3), (1, 1), (0, 2), (1, 3), (1, 2)):
                arrived(h, u, d)
                for e in (1, 3, 2):
                    spread(u, across(u, d), across(1 - u, e), group_sem.at[h, d])
        else:
            for u in range(2):
                out[half_rows(u), :] = finished(u)

    owned = out[...]
    top_row = pl.ds(0, 1)
    col_tot[q, top_row, :] = jnp.sum(owned * owned, axis=0, keepdims=True)

    far_first = (8, 7, 9, 6, 10, 5, 11, 4, 12, 3, 13, 2, 14, 1, 15)
    for stage, (tot, me) in enumerate(((col_tot, q), (row_tot, p))):
        for d in far_first:
            device = (p, (q + d) % NCOL) if stage == 0 else ((p + d) % NROW, q)
            remote(tot.at[me, top_row], tot.at[me, top_row], tot_sem.at[0, stage], tot_sem.at[1, stage], device).start()
        every = tot.at[pl.ds(0, 15), top_row]
        remote(every, every, tot_sem.at[0, stage], tot_sem.at[1, stage], (p, z * 2 + other)).wait()
        if stage == 0:
            row_tot[p, top_row, :] = jnp.sum(col_tot[:, top_row, :], axis=0)
    totals = jnp.sum(row_tot[:, top_row, :], axis=0)
    out[...] = owned * lax.rsqrt(totals / ENTITIES + 1e-06)
    for h in range(HOPS):
        sent(2, h, cross.at[0, pl.ds(0, 7)])
    for h in range(HOPS - 1):
        sent(1, h, state.at[0, pl.ds(0, NROW - 1)])


def run_chain(table, first, cells):
    vmem = pl.BlockSpec(memory_space=pltpu.VMEM)
    hbm = pl.BlockSpec(memory_space=pltpu.HBM)
    return pl.pallas_call(
        chain_kernel,
        out_shape=jax.ShapeDtypeStruct((BLOCK, QUERIES), F32),
        in_specs=[hbm] * 3,
        out_specs=vmem,
        scratch_shapes=[
            pltpu.SMEM((HOPS * 8, 128), jnp.int32),
            pltpu.VMEM((SLOTS + 1, TILE, 2 * TILE), F32),
            pltpu.VMEM((SLOTS + 1, TILE, 2 * TILE), F32),
            pltpu.VMEM((NROW, NCOL * BLOCK, BLOCK), BF16),
            pltpu.VMEM((NROW, NCOL * BLOCK, BLOCK), BF16),
            pltpu.VMEM((NY * BLOCK, 2 * QUERIES), BF16),
            pltpu.VMEM((NCOL, BLOCK, QUERIES), F32),
            pltpu.VMEM((HOPS, NZ, BLOCK, QUERIES), F32),
            pltpu.VMEM((HOPS, 2, 4, BLOCK, QUERIES), F32),
            pltpu.VMEM((HOPS - 1, NROW, BLOCK, QUERIES), F32),
            pltpu.VMEM((NCOL, 8, QUERIES), F32),
            pltpu.VMEM((NROW, 8, QUERIES), F32),
            pltpu.SemaphoreType.DMA((4,)),
            pltpu.SemaphoreType.DMA((3, HOPS)),
            pltpu.SemaphoreType.DMA((HOPS, NZ)),
            pltpu.SemaphoreType.DMA((HOPS, 2, 4, 2)),
            pltpu.SemaphoreType.DMA((HOPS - 1, 2, NX - 1)),
            pltpu.SemaphoreType.DMA((HOPS - 1, NX)),
            pltpu.SemaphoreType.DMA((2, 2)),
        ],
        compiler_params=pltpu.CompilerParams(
            collective_id=0, has_side_effects=True, vmem_limit_bytes=60 * 2**20
        ),
        name="relation_chain",
    )(table, first, cells)


def shards(tiles, tile_coords, tile_count, seeds, chain):
    cells, table, product = merge(
        chain, tile_count[0, 0], tile_coords[0, 0], seeds.reshape(1, QUERIES), tiles[0, 0]
    )
    return run_chain(table, product.reshape(NCOL, BLOCK, QUERIES), cells)


def solution(mesh):
    in_specs = (
        P("row", "col", None, None, None, None),
        P("row", "col", None, None, None),
        P("row", "col", None),
        P(),
        P(),
    )
    out_specs = P(("row", "col"), None)
    return jax.shard_map(shards, mesh=mesh, in_specs=in_specs, out_specs=out_specs, check_vma=False)
```
